512 devices in a mesh: lat: 8 (over z_lo, core), lon: 64 (over z_hi, x, y).
Axes of the slice: x: 4, y: 8, z: 8 (z_hi: 2, z_lo: 4; z = z_hi * 4 + z_lo), core: 2. Of those that a mesh axis runs over, the one named last changes fastest.
Arguments:
- background_state: bfloat16 [18, 5760, 1024], P(None, 'lon', 'lat'), may hold values from -6 to 6
- perturbation: bfloat16 [18, 5760, 1024], P(None, 'lon', 'lat'), may hold values from -16 to 16
- surface_pattern_index: int32 [5760, 1024], P('lon', 'lat'), may hold values from 0 to 15
- surface_amplitude_table: float32 [16], replicated, may hold values from -4 to 4
- cutoff: int32 [1024], P('lat'), may hold values from 4 to 64, as said below
- zonal_row_weight: float32 [1024], P('lat'), may hold values from 0.5 to 2
- diffusivity: float32 [18], replicated, may hold values from 0.04 to 0.25
- input_weight: bfloat16 [48, 18], replicated, may hold values from -1.5 to 1.5
- bias: float32 [48], replicated, may hold values from -4 to 4
- output_weight: float32 [18, 48], replicated, may hold values from -0.875 to 0.875
Outputs:
- tangent: bfloat16 [18, 5760, 1024], P(None, 'lon', 'lat')
- gradient: bfloat16 [18, 5760, 1024], P(None, 'lon', 'lat')
The draws below stay inside these ranges and needn't reach their ends.
Inputs may be any that keep to these rules, and one draw needn't show every extreme that they name: Rows 64 or more rows away from both ends of the grid have cutoff 64; the first and last rows have cutoff 4; a row d < 64 rows from the nearer end has cutoff at least 4 + (d * 60) // 64.
All inputs are finite; a program needn't handle non-finite values.
Results may differ from the reference program's by a relative error of at most 0.001.
Values sent between devices are 32-bit elements; how exact they have to be, the bound alone decides.
A program may use at most 64 MiB of HBM per device.

```python
import math
import jax
import jax.numpy as jnp
from jax import lax

C = 18
LONGITUDE_COUNT = 5760
LATITUDE_ROWS = 1024
HID = 48
KW = 64
CUT_MIN = 4
POLAR = 64
SURFACE_PATTERNS = 16


def draw_cutoff(key, part):
    rows_index = jnp.arange(LATITUDE_ROWS, dtype=jnp.int32)
    distance = jnp.minimum(rows_index, LATITUDE_ROWS - 1 - rows_index)
    jitter = jax.random.randint(key, (LATITUDE_ROWS,), 0, 4)
    base_cut = CUT_MIN + distance * (KW - CUT_MIN) // POLAR
    cut_value = jnp.minimum(base_cut + jitter * (distance > 0).astype(jnp.int32), KW)
    return jnp.where(distance < POLAR, cut_value, KW).astype(jnp.int32)


def draw_perturbation(key, part):
    subkeys = jax.random.split(key, 9)
    full_shape = (C, LONGITUDE_COUNT, LATITUDE_ROWS)
    rough_part = jnp.clip(jax.random.normal(subkeys[0], full_shape, jnp.float32), -5.0, 5.0)
    strength = 0.5
    longitudes = jnp.arange(LONGITUDE_COUNT, dtype=jnp.int32)[None, :, None]
    combined = rough_part
    for wave_index in range(4):
        wave_numbers = jax.random.randint(subkeys[1 + 2 * wave_index], (C, 1, LATITUDE_ROWS), 1, KW + 1)
        amp_phase = jnp.clip(jax.random.normal(subkeys[2 + 2 * wave_index], (2, C, 1, LATITUDE_ROWS), jnp.float32), -3.0, 3.0)
        phase_index = wave_numbers * longitudes % LONGITUDE_COUNT
        angles = phase_index.astype(jnp.float32) * (2.0 * math.pi / LONGITUDE_COUNT) + 3.0 * amp_phase[1]
        combined = combined + strength * amp_phase[0] * jnp.cos(angles)
    return combined.astype(jnp.bfloat16)


def touch_ends(values, rng, low, top_value):
    longest = values.shape.index(max(values.shape))
    spots = []
    for shift in (0, 1):
        where = [jax.random.randint(jax.random.fold_in(rng, axis), (), 0, length) for axis, length in enumerate(values.shape)]
        where[longest] = (where[longest] + shift) % values.shape[longest]
        spots.append(tuple(where))
    return values.at[spots[0]].set(low).at[spots[1]].set(top_value)


def levels(rng, extent, shards, smallest, top_value):
    gain = 1.0
    for position, parts in shards:
        draws = jax.random.uniform(jax.random.fold_in(jax.random.fold_in(rng, 6), position), (parts,), jnp.float32, smallest / len(shards), top_value / len(shards))
        gain = gain * jnp.repeat(jnp.exp(draws), extent[position] // parts).reshape((-1,) + (1,) * (len(extent) - 1 - position))
    return gain


def gaussian(stream_key, dims, deviation, bound, cuts=(), held_as=jnp.bfloat16):
    level = levels(stream_key, dims, cuts, -0.22, 0.18) if cuts else 1.0
    array = jax.random.normal(stream_key, dims, jnp.float32) * deviation * level
    return jnp.minimum(jnp.maximum(array, -bound), bound).astype(held_as)


def setup_inputs(seed: int = 0) -> dict:
    arg_keys = jax.random.split(jax.random.key(seed), 11)
    return {
        "background_state": gaussian(arg_keys[0], (C, LONGITUDE_COUNT, LATITUDE_ROWS), 1.0, 6.0, ((1, 64), (2, 8))),
        "perturbation": draw_perturbation(jax.random.fold_in(arg_keys[10], 71), 0),
        "surface_pattern_index": touch_ends(jax.random.randint(arg_keys[2], (LONGITUDE_COUNT, LATITUDE_ROWS), 0, SURFACE_PATTERNS), jax.random.fold_in(arg_keys[2], 1), 0, SURFACE_PATTERNS - 1).astype(jnp.int32),
        "surface_amplitude_table": gaussian(arg_keys[3], (SURFACE_PATTERNS,), 1.0, 4.0, (), jnp.float32),
        "cutoff": draw_cutoff(jax.random.fold_in(arg_keys[10], 71), 0),
        "zonal_row_weight": jnp.clip(jnp.exp(math.log(2.0) - 1.3862944 * jax.random.uniform(arg_keys[5], (LATITUDE_ROWS,), jnp.float32) ** levels(arg_keys[5], (LATITUDE_ROWS,), ((0, 8),), -0.2, 0.2)), 0.5, 2.0),
        "diffusivity": jnp.clip(jnp.exp(jax.random.uniform(arg_keys[6], (C,), jnp.float32, math.log(0.04), math.log(0.25))), 0.04, 0.25),
        "input_weight": gaussian(arg_keys[7], (HID, C), C ** -0.5, 1.5),
        "bias": gaussian(arg_keys[8], (HID,), 1.0, 4.0, (), jnp.float32),
        "output_weight": gaussian(arg_keys[9], (C, HID), HID ** -0.5, 0.875, (), jnp.float32),
    }


TOP_PRECISION = lax.Precision.HIGHEST


def spectral_table(longitudes):
    wave_numbers = jnp.arange(1, KW + 1, dtype=jnp.int32)
    phase_index = (longitudes[:, None] * wave_numbers[None, :]) % LONGITUDE_COUNT
    angles = phase_index.astype(jnp.float32) * (2.0 * math.pi / LONGITUDE_COUNT)
    return jnp.concatenate([jnp.cos(angles), jnp.sin(angles)], axis=1)


def removal_weights(cutoff):
    wave_numbers = jnp.arange(1, KW + 1, dtype=jnp.float32)[:, None]
    cut_limit = cutoff.astype(jnp.float32)[None, :]
    cut_ratio = cut_limit / wave_numbers
    damping = jnp.where(wave_numbers > cut_limit, 1.0 - cut_ratio * cut_ratio, 0.0)
    return jnp.concatenate([damping, damping], axis=0)


def polar_filter(state_grid_field, weight_set, fourier_basis_table):
    fourier_spectra = jnp.einsum("hpu,pa->hau", state_grid_field, fourier_basis_table, precision=TOP_PRECISION)
    removed_part = jnp.einsum("zum,gu->zgm", fourier_spectra * weight_set[None], fourier_basis_table, precision=TOP_PRECISION)
    return state_grid_field - removed_part * (2.0 / LONGITUDE_COUNT)


def diffuse(state_grid_field, diffusivity, zonal_row_weight):
    zonal_term = jnp.roll(state_grid_field, 1, axis=1) + jnp.roll(state_grid_field, -1, axis=1) - 2.0 * state_grid_field
    padded = jnp.pad(state_grid_field, ((0, 0), (0, 0), (1, 1)))
    meridional = padded[:, :, 2:] + padded[:, :, :-2] - 2.0 * state_grid_field
    return diffusivity[:, None, None] * (zonal_row_weight[None, None, :] * zonal_term + meridional)


def blockwise(function, background_state, other):
    block_count = 16

    def split_lon(values_in):
        shaped = values_in.reshape(values_in.shape[0], block_count, values_in.shape[1] // block_count, values_in.shape[2])
        return jnp.moveaxis(shaped, 1, 0)

    result = lax.map(lambda pieces: function(pieces[0], pieces[1]), (split_lon(background_state), split_lon(other)))
    result = jnp.moveaxis(result, 0, 1)
    return result.reshape(result.shape[0], block_count * result.shape[2], result.shape[3])


def reference(background_state, perturbation, surface_pattern_index, surface_amplitude_table, cutoff, zonal_row_weight, diffusivity, input_weight, bias, output_weight):
    wide_weight = input_weight.astype(jnp.float32)

    def slope_function(background_block):
        before_activation = jnp.einsum("vb,bqf->vqf", wide_weight, background_block.astype(jnp.float32), precision=TOP_PRECISION)
        active = jnp.tanh(before_activation + bias[:, None, None])
        return 1.0 - active * active

    def forward_block(background_block, perturbation_block):
        hidden_forward = jnp.einsum("vb,bqf->vqf", wide_weight, perturbation_block, precision=TOP_PRECISION) * slope_function(background_block)
        return jnp.einsum("sm,mxq->sxq", output_weight, hidden_forward, precision=TOP_PRECISION)

    def adjoint_block(background_block, backward_block):
        hidden_backward = jnp.einsum("xf,xbe->fbe", output_weight, backward_block, precision=TOP_PRECISION) * slope_function(background_block)
        return jnp.einsum("zo,zmf->omf", wide_weight, hidden_backward, precision=TOP_PRECISION)

    surface_field = surface_amplitude_table[surface_pattern_index]
    start_pert = perturbation.astype(jnp.float32)
    perturbation_field = jnp.concatenate([start_pert[:1] + surface_field[None], start_pert[1:]], axis=0)
    weight_set = removal_weights(cutoff)
    fourier_basis_table = spectral_table(jnp.arange(LONGITUDE_COUNT, dtype=jnp.int32))
    tangent_image = perturbation_field + diffuse(perturbation_field, diffusivity, zonal_row_weight) + 0.5 * blockwise(forward_block, background_state, perturbation_field)
    tangent_full = polar_filter(tangent_image, weight_set, fourier_basis_table)
    adjoint_input = polar_filter(tangent_full, weight_set, fourier_basis_table)
    gradient = adjoint_input + diffuse(adjoint_input, diffusivity, zonal_row_weight) + 0.5 * blockwise(adjoint_block, background_state, adjoint_input)
    return tangent_full.astype(jnp.bfloat16), gradient.astype(jnp.bfloat16)
```

```python
import functools
import math

import jax
import jax.numpy as jnp
import numpy as np
from jax import lax
from jax.experimental import pallas as pl
from jax.experimental.pallas import tpu as pltpu
from jax.sharding import PartitionSpec as P

LONGITUDE_COUNT = 5760
C = 18
HID = 48
L = 90
LP = 96
R = 128
KW = 64
N_LON = 64
N_LAT = 8
F32 = jnp.float32
BF16 = jnp.bfloat16
MESH = pl.DeviceIdType.MESH

WIDTH = [min(64, -(-(8 * a + 4) * 16 // 15)) for a in range(8)]
FOLD = []
for kind in (0, 1):
    FOLD += [((kind, 7), None), ((kind, 6), (kind, 0)), ((kind, 5), (kind, 1)), ((kind, 4), (kind, 2))]
FOLD.append(((0, 3), (1, 3)))
PAIRS = C // 2
PER_OWNER = 2
TILES = PAIRS * len(FOLD)
OWNERS = -(-TILES // PER_OWNER)
SLOTS = OWNERS * PER_OWNER


def base_tables():
    wave = np.arange(1, KW + 1)
    rows = np.zeros((2, LP, 2 * KW), np.float64)
    for row in range(LP):
        if row <= L or row == LP - 1:
            angle = 2 * math.pi * (((row if row <= L else -1) * wave) % LONGITUDE_COUNT) / LONGITUDE_COUNT
            rows[0, row] = np.concatenate([np.cos(angle)] * 2)
            rows[1, row] = np.concatenate([np.sin(angle)] * 2)
    turn = np.zeros((N_LON, 2, 2 * KW), np.float64)
    for p in range(N_LON):
        angle = 2 * math.pi * ((p * L * wave) % LONGITUDE_COUNT) / LONGITUDE_COUNT
        turn[p, 0] = np.concatenate([np.cos(angle), np.sin(angle)])
        turn[p, 1] = np.concatenate([-np.sin(angle), np.cos(angle)])
    return rows.astype(np.float32), turn.astype(np.float32)


def iota(shape, dim):
    return lax.broadcasted_iota(jnp.int32, shape, dim)


def one_hot(mask):
    return jnp.where(mask, 1.0, 0.0).astype(BF16)


def dot(a, b):
    return lax.dot_general(a, b, (((1,), (0,)), ((), ())), preferred_element_type=F32)


def dot_nt(a, b, precision=None):
    return lax.dot_general(a, b, (((1,), (1,)), ((), ())), preferred_element_type=F32, precision=precision)


def split(x):
    high = x.astype(BF16)
    return high, (x - high.astype(F32)).astype(BF16)


def is_polar():
    lat = lax.axis_index("lat")
    return (lat == 0) | (lat == N_LAT - 1)


def polar_row(d):
    return jnp.where(lax.axis_index("lat") == N_LAT - 1, R - 1 - d, d)


def pair_select():
    row, col = iota((2 * R, R), 0), iota((2 * R, R), 1)
    return one_hot(((row >> 7) == (col >> 6)) & ((row & 127) == polar_row(col & 63)))


def pair_select_back():
    row, col = iota((R, 2 * R), 0), iota((R, 2 * R), 1)
    return one_hot(((col >> 7) == (row >> 6)) & ((col & 127) == polar_row(row & 63)))


def basis(base_ref, turn_ref):
    p = lax.axis_index("lon")
    turn = turn_ref[p]
    return base_ref[0] * turn[0:1, :] + base_ref[1] * turn[1:2, :]


def pack16(x):
    n = x.shape[0] * 8
    return jnp.concatenate([x[:, :8, :].reshape(n, R), x[:, 8:, :].reshape(n, R)], axis=1)


def spread_rows(n):
    return one_hot((iota((8 * n, n), 0) >> 3) == iota((8 * n, n), 1))


def spread_cols(n):
    return one_hot((iota((n, 8 * n), 1) >> 3) == iota((n, 8 * n), 0))


def diag8(x):
    return jnp.where((iota(x.shape, 0) & 7) == (iota(x.shape, 1) & 7), x, 0.0).astype(BF16)


def diffusion(x, zonal_weight, d, lane):
    zonal = pltpu.roll(x, 1, 0) + pltpu.roll(x, LP - 1, 0) - 2.0 * x
    east = jnp.where(lane == R - 1, 0.0, pltpu.roll(x, R - 1, 1))
    west = jnp.where(lane == 0, 0.0, pltpu.roll(x, 1, 1))
    return zonal_weight * zonal + east + west - 2.0 * x


def forward_kernel(
    table_ref, diff_ref, bias_ref, bg_ref, pert_ref, index_ref, zonal_ref, win_ref, wout_ref, base_ref, turn_ref,
    image_ref, slope_ref, spec_ref, lonmsg_ref, latmsg_ref,
    pf, bf, bias_tile, a_in, a_out,
):
    surf = jnp.zeros((L, R), F32)
    index = index_ref[...]
    for s in range(16):
        surf = jnp.where(index == s, table_ref[s], surf)
    pf[:, 0:L, :] = pert_ref[...].astype(F32)
    pf[0, 0:L, :] = pert_ref[0].astype(F32) + surf
    pf[:, L:LP, :] = jnp.zeros((C, LP - L, R), F32)
    bf[:, 0:L, :] = bg_ref[...].astype(F32)
    bf[:, L:LP, :] = jnp.zeros((C, LP - L, R), F32)
    for h in range(HID):
        bias_tile[8 * h : 8 * h + 8, :] = jnp.full((8, R), bias_ref[h], F32)

    col = iota((C, 160), 1)
    cols_in = one_hot(jnp.where(col < 144, col >> 3, 0) == iota((C, 160), 0))
    a_in[...] = diag8(dot(dot(spread_rows(HID), win_ref[...]).astype(BF16), cols_in))
    for i, part in enumerate(split(0.5 * wout_ref[...])):
        a_out[i] = diag8(dot(dot(spread_rows(C), part).astype(BF16), spread_cols(HID)))

    lane = iota((LP, R), 1)
    zonal_weight = zonal_ref[...]

    def base(c, carry):
        x = pf[c]
        d = diff_ref[c]
        image_ref[c] = x + d * diffusion(x, zonal_weight, d, lane)
        return carry

    lax.fori_loop(0, C, base, 0)

    def columns(p, carry):
        start = pl.multiple_of(p * 16, 16)
        xb = pack16(bf[:, pl.ds(start, 16), :]).astype(BF16)
        xb = jnp.concatenate([xb, jnp.zeros((16, 2 * R), BF16)], axis=0)
        pre = dot(a_in[...], xb)
        b = bias_tile[...]
        active = jnp.tanh(pre + jnp.concatenate([b, b], axis=1))
        slope = 1.0 - active * active
        slope_ref[:, pl.ds(start, 8), :] = slope[:, :R].reshape(HID, 8, R)
        slope_ref[:, pl.ds(start + 8, 8), :] = slope[:, R:].reshape(HID, 8, R)
        xp = pack16(pf[:, pl.ds(start, 16), :])
        top = xp[0:8]
        rest = top - top.astype(BF16).astype(F32)
        last = rest - rest.astype(BF16).astype(F32)
        xp = jnp.concatenate([xp, rest, last], axis=0).astype(BF16)
        high, low = split(slope * dot(a_in[...], xp))
        part = dot(a_out[0], high) + dot(a_out[0], low) + dot(a_out[1], high)
        image_ref[:, pl.ds(start, 8), :] += part[:, :R].reshape(C, 8, R)
        image_ref[:, pl.ds(start + 8, 8), :] += part[:, R:].reshape(C, 8, R)
        return carry

    lax.fori_loop(0, LP // 16, columns, 0)

    row8, lane8 = iota((8, R), 0), iota((8, R), 1)
    edge = ((lane8 == 0) & (row8 < 2)) | ((lane8 == R - 1) & (row8 >= 2) & (row8 < 4))
    pick_image = jnp.where(edge & ((row8 & 1) == 0), 1.0, 0.0)
    pick_pert = jnp.where(edge & ((row8 & 1) == 1), 1.0, 0.0)
    top = lax.Precision.HIGHEST
    for c in range(C):
        x = image_ref[c]
        lonmsg_ref[0, 0, c : c + 1, :] = x[0:1, :]
        lonmsg_ref[0, 1, c : c + 1, :] = x[LP - 1 : LP, :]
        lonmsg_ref[1, 0, c : c + 1, :] = x[L - 1 : L, :]
        lonmsg_ref[1, 1, c : c + 1, :] = x[L : L + 1, :]
        cut = dot_nt(pick_image, x, top) + dot_nt(pick_pert, diff_ref[c] * pf[c], top)
        for e in range(4):
            latmsg_ref[e // 2, e % 2, c : c + 1, 0:LP] = cut[e : e + 1, :]

    @pl.when(is_polar())
    def _():
        b = basis(base_ref, turn_ref)
        bt = jnp.concatenate([b, jnp.zeros((R - LP, R), F32)], axis=0).T
        bt_high, bt_low = split(bt[:, :LP])
        select = pair_select()
        lane64 = iota((8, R), 1) & 63

        def spectra(q, carry):
            x = jnp.concatenate([image_ref[2 * q], image_ref[2 * q + 1]], axis=1)
            high, low = split(x)
            high = dot(high, select).astype(BF16)
            low = dot(low, select).astype(BF16)
            s = dot(bt_high, high) + dot(bt_high, low) + dot(bt_low, high)
            for i, (big, small) in enumerate(FOLD):
                at = 64 * big[0] + 8 * big[1]
                tile = s[at : at + 8, :]
                if small is not None:
                    at = 64 * small[0] + 8 * small[1]
                    moved = pltpu.roll(s[at : at + 8, :], 64 - WIDTH[small[1]], 1)
                    tile = jnp.where(lane64 < WIDTH[big[1]], tile, moved)
                spec_ref[q * len(FOLD) + i] = tile
            return carry

        lax.fori_loop(0, PAIRS, spectra, 0)
        for i in range(TILES, SLOTS):
            spec_ref[i] = jnp.zeros((8, R), F32)


def exchange_kernel(
    spec_ref, lonmsg_ref, latmsg_ref, full_ref, lonrecv_ref, latrecv_ref,
    parts, total, send_sem, lon_sem, lat_sem, rs_sem, ag_sem, own_sem,
):
    lat, lon = lax.axis_index("lat"), lax.axis_index("lon")
    polar = is_polar()
    owner = lon < OWNERS
    barrier = pltpu.get_barrier_semaphore()
    left, right = lax.rem(lon + N_LON - 1, N_LON), lax.rem(lon + 1, N_LON)
    around = (left, lon, right)

    def greet(lat_to, lon_to):
        pl.semaphore_signal(barrier, inc=1, device_id=(lat_to, lon_to), device_id_type=MESH)

    @pl.when(polar & owner)
    def _():
        def tell(d, carry):
            greet(lat, lax.rem(lon + d, N_LON))
            return carry

        lax.fori_loop(1, N_LON, tell, 0)

    greet(lat, left)
    greet(lat, right)

    @pl.when(lat > 0)
    def _():
        for to in around:
            greet(lat - 1, to)

    @pl.when(lat < N_LAT - 1)
    def _():
        for to in around:
            greet(lat + 1, to)

    sides = (lat > 0).astype(jnp.int32) + (lat < N_LAT - 1).astype(jnp.int32)
    owners = polar.astype(jnp.int32) * (OWNERS - owner.astype(jnp.int32))
    pl.semaphore_wait(barrier, 2 + 3 * sides + owners)

    def remote(src, dst, send, recv, lat_to, lon_to):
        return pltpu.make_async_remote_copy(
            src_ref=src, dst_ref=dst, send_sem=send, recv_sem=recv, device_id=(lat_to, lon_to), device_id_type=MESH
        )

    def wait(ref, sem):
        pltpu.make_async_copy(ref, ref, sem).wait()

    @pl.when(polar)
    def _():
        def scatter(o, carry):
            @pl.when(o != lon)
            def _():
                remote(spec_ref.at[o], parts.at[lon], send_sem.at[0], rs_sem, lat, o).start()

            return carry

        lax.fori_loop(0, OWNERS, scatter, 0)

        @pl.when(owner)
        def _():
            pltpu.make_async_copy(spec_ref.at[lon], parts.at[lon], own_sem.at[0]).start()

    remote(lonmsg_ref.at[1], lonrecv_ref.at[0], send_sem.at[1], lon_sem, lat, right).start()
    remote(lonmsg_ref.at[0], lonrecv_ref.at[1], send_sem.at[1], lon_sem, lat, left).start()

    @pl.when(lat > 0)
    def _():
        for i, to in enumerate(around):
            remote(latmsg_ref.at[0], latrecv_ref.at[1, 2 - i], send_sem.at[2], lat_sem.at[1], lat - 1, to).start()

    @pl.when(lat < N_LAT - 1)
    def _():
        for i, to in enumerate(around):
            remote(latmsg_ref.at[1], latrecv_ref.at[0, 2 - i], send_sem.at[3], lat_sem.at[0], lat + 1, to).start()

    @pl.when(polar & owner)
    def _():
        wait(parts.at[pl.ds(0, N_LON - 1)], rs_sem)
        wait(parts.at[0], own_sem.at[0])

        def add(i, acc):
            return acc + parts[i]

        total[...] = lax.fori_loop(0, N_LON, add, jnp.zeros((PER_OWNER, 8, R), F32))

        def gather(d, carry):
            remote(total, full_ref.at[lon], send_sem.at[4], ag_sem, lat, lax.rem(lon + d, N_LON)).start()
            return carry

        lax.fori_loop(1, N_LON, gather, 0)
        pltpu.make_async_copy(total, full_ref.at[lon], own_sem.at[1]).start()
        wait(full_ref.at[pl.ds(0, OWNERS - 1)], ag_sem)
        wait(total, own_sem.at[1])
        wait(parts.at[pl.ds(0, N_LON - 1)], send_sem.at[4])
        wait(full_ref.at[pl.ds(0, OWNERS - 1)], send_sem.at[0])

    @pl.when(polar & jnp.logical_not(owner))
    def _():
        wait(full_ref, ag_sem)
        wait(full_ref, send_sem.at[0])

    wait(lonrecv_ref, lon_sem)
    wait(lonrecv_ref, send_sem.at[1])

    @pl.when(lat > 0)
    def _():
        wait(latrecv_ref.at[0], lat_sem.at[0])
        wait(latrecv_ref.at[0], send_sem.at[2])

    @pl.when(lat < N_LAT - 1)
    def _():
        wait(latrecv_ref.at[1], lat_sem.at[1])
        wait(latrecv_ref.at[1], send_sem.at[3])


def adjoint_kernel(
    diff_ref, image_ref, slope_ref, full_ref, lonrecv_ref, latrecv_ref, latmsg_ref, cutoff_ref, zonal_ref,
    win_ref, wout_ref, base_ref, turn_ref, tangent_ref, gradient_ref,
    adj, part_ref, a_back, a_in, corr,
):
    lat = lax.axis_index("lat")
    part = split(0.5 * wout_ref[...])
    col_c = spread_cols(C)
    for i in range(2):
        a_back[i] = diag8(dot(dot_nt(spread_rows(HID), part[i]).astype(BF16), col_c))
    a_in[...] = diag8(dot(dot_nt(spread_rows(C), win_ref[...]).astype(BF16), spread_cols(HID)))

    lane24 = iota((24, R), 1)
    live = iota((24, R), 0) < C

    def edge(side, own):
        image, pert = [[latrecv_ref[side, i, kind] for i in range(3)] for kind in range(2)]
        fix = jnp.where(lane24 < L, pert[1], 0.0)
        fix = jnp.where(lane24 == L, pltpu.roll(pert[2], L, 1), fix)
        fix = jnp.where(lane24 == LP - 1, pltpu.roll(pert[0], LP - L, 1), fix)
        halo = image[1] + own
        halo = halo + jnp.where(lane24 == 0, pltpu.roll(image[0], R - L, 1), 0.0)
        halo = halo + jnp.where(lane24 == L - 1, pltpu.roll(image[2], R - (LP - L), 1), 0.0)
        halo = jnp.where(lane24 < L, halo, 0.0)
        there = (lat > 0) if side == 0 else (lat < N_LAT - 1)
        return jnp.where(live & there, fix, 0.0), jnp.where(live & there, halo, 0.0)

    down_fix, down_halo = edge(0, latmsg_ref[0, 1])
    up_fix, up_halo = edge(1, latmsg_ref[1, 1])
    corr[...] = jnp.concatenate([down_fix, up_fix, down_halo, up_halo, jnp.zeros((32, R), F32)], axis=0).T

    lane = iota((LP, R), 1)
    row8 = iota((8, R), 0)

    def at_edges(c, first):
        low = corr[0:LP, first + c : first + c + 1]
        high = corr[0:LP, first + 24 + c : first + 25 + c]
        return jnp.where(lane == 0, low, jnp.where(lane == R - 1, high, 0.0))

    for c in range(C):
        adj[c] = image_ref[c] + at_edges(c, 0)
        adj[c, 0:8, :] += jnp.where(row8 == 0, lonrecv_ref[0, 1, c : c + 1, :], 0.0)
        end = jnp.where(row8 == 1, lonrecv_ref[1, 1, c : c + 1, :], 0.0)
        end = jnp.where(row8 == 2, lonrecv_ref[1, 0, c : c + 1, :], end)
        end = jnp.where(row8 == 7, lonrecv_ref[0, 0, c : c + 1, :], end)
        adj[c, LP - 8 : LP, :] += end

    @pl.when(jnp.logical_not(is_polar()))
    def _():
        tangent_ref[...] = adj[:, 0:L, :].astype(BF16)

    @pl.when(is_polar())
    def _():
        row, col = iota((R, R), 0), iota((R, R), 1)
        pick = one_hot(row == polar_row(col & 63))
        cut = dot(jnp.broadcast_to(cutoff_ref[...].astype(F32), (8, R)).astype(BF16), pick)[0:1, :]
        wave = ((row & 63) + 1).astype(F32)
        ratio = cut / wave
        g = jnp.where(wave > cut, 1.0 - ratio * ratio, 0.0)
        g_tangent = g * (2.0 / LONGITUDE_COUNT)
        g_adjoint = g_tangent * (2.0 - g)
        b_high, b_low = split(basis(base_ref, turn_ref))
        back = pair_select_back()

        def rebuild(q, carry):
            tiles = {}
            for i, (big, small) in enumerate(FOLD):
                tile = full_ref[q * len(FOLD) + i]
                tiles[big] = tile
                if small is not None:
                    tiles[small] = pltpu.roll(tile, R - 64 + WIDTH[small[1]], 1)
            s = jnp.concatenate([tiles[kind, a] for kind in (0, 1) for a in range(8)], axis=0)
            high, low = split(jnp.concatenate([g_tangent * s, g_adjoint * s], axis=1))
            removed = dot(b_high, high) + dot(b_high, low) + dot(b_low, high)
            removed = jnp.concatenate([removed[:, :R], removed[:, R:]], axis=0)
            high, low = split(removed)
            removed = dot(high, back) + dot(low, back)
            for h in range(2):
                c = 2 * q + h
                x = adj[c]
                lanes = slice(h * R, (h + 1) * R)
                tangent_ref[c] = (x - removed[:LP, lanes])[0:L].astype(BF16)
                adj[c] = x - removed[LP:, lanes]
            return carry

        lax.fori_loop(0, PAIRS, rebuild, 0)

    def columns(p, carry):
        start = pl.multiple_of(p * 16, 16)
        high, low = split(pack16(adj[:, pl.ds(start, 16), :]))
        hidden = dot(a_back[0], high) + dot(a_back[0], low) + dot(a_back[1], high)
        high, low = split(hidden * pack16(slope_ref[:, pl.ds(start, 16), :]))
        part = dot(a_in[...], high) + dot(a_in[...], low)
        part_ref[:, pl.ds(start, 8), :] = part[:, :R].reshape(C, 8, R)
        part_ref[:, pl.ds(start + 8, 8), :] = part[:, R:].reshape(C, 8, R)
        return carry

    lax.fori_loop(0, LP // 16, columns, 0)

    zonal_weight = zonal_ref[...]
    for c in range(C):
        x = adj[c]
        d = diff_ref[c]
        out = x + d * (diffusion(x, zonal_weight, d, lane) + at_edges(c, 48)) + part_ref[c]
        gradient_ref[c] = out[0:L].astype(BF16)


def vmem():
    return pl.BlockSpec(memory_space=pltpu.VMEM)


def smem():
    return pl.BlockSpec(memory_space=pltpu.SMEM)


def anywhere():
    return pl.BlockSpec(memory_space=pl.ANY)


LIMIT = 48 * 2**20


def per_device(
    background_state,
    perturbation,
    surface_pattern_index,
    surface_amplitude_table,
    cutoff,
    zonal_row_weight,
    diffusivity,
    input_weight,
    bias,
    output_weight,
):
    base, turn = (jnp.asarray(t) for t in base_tables())
    zonal = zonal_row_weight.reshape(1, R)
    message = jax.ShapeDtypeStruct((2, 2, 24, R), F32)
    image, slope, spec, lonmsg, latmsg = pl.pallas_call(
        forward_kernel,
        out_shape=(
            jax.ShapeDtypeStruct((C, LP, R), F32),
            jax.ShapeDtypeStruct((HID, LP, R), F32),
            jax.ShapeDtypeStruct((SLOTS, 8, R), F32),
            message,
            message,
        ),
        in_specs=[smem()] * 3 + [vmem()] * 8,
        out_specs=(vmem(),) * 5,
        scratch_shapes=[
            pltpu.VMEM((C, LP, R), F32),
            pltpu.VMEM((C, LP, R), F32),
            pltpu.VMEM((8 * HID, R), F32),
            pltpu.VMEM((8 * HID, 160), BF16),
            pltpu.VMEM((2, 8 * C, 8 * HID), BF16),
        ],
        compiler_params=pltpu.CompilerParams(vmem_limit_bytes=LIMIT),
        name="forward",
    )(
        surface_amplitude_table, diffusivity, bias, background_state, perturbation, surface_pattern_index, zonal,
        input_weight, output_weight, base, turn,
    )
    full, lonrecv, latrecv = pl.pallas_call(
        exchange_kernel,
        out_shape=(
            jax.ShapeDtypeStruct((OWNERS, PER_OWNER, 8, R), F32),
            message,
            jax.ShapeDtypeStruct((2, 3, 2, 24, R), F32),
        ),
        in_specs=[anywhere()] * 3,
        out_specs=(anywhere(),) * 3,
        scratch_shapes=[
            pltpu.VMEM((N_LON, PER_OWNER, 8, R), F32),
            pltpu.VMEM((PER_OWNER, 8, R), F32),
            pltpu.SemaphoreType.DMA((5,)),
            pltpu.SemaphoreType.DMA,
            pltpu.SemaphoreType.DMA((2,)),
            pltpu.SemaphoreType.DMA,
            pltpu.SemaphoreType.DMA,
            pltpu.SemaphoreType.DMA((2,)),
        ],
        compiler_params=pltpu.CompilerParams(collective_id=0, has_side_effects=True, vmem_limit_bytes=LIMIT // 4),
        name="exchange",
    )(spec.reshape(OWNERS, PER_OWNER, 8, R), lonmsg, latmsg)
    return pl.pallas_call(
        adjoint_kernel,
        out_shape=(jax.ShapeDtypeStruct((C, L, R), BF16), jax.ShapeDtypeStruct((C, L, R), BF16)),
        in_specs=[smem()] + [vmem()] * 12,
        out_specs=(vmem(), vmem()),
        scratch_shapes=[
            pltpu.VMEM((C, LP, R), F32),
            pltpu.VMEM((C, LP, R), F32),
            pltpu.VMEM((2, 8 * HID, 8 * C), BF16),
            pltpu.VMEM((8 * C, 8 * HID), BF16),
            pltpu.VMEM((R, R), F32),
        ],
        compiler_params=pltpu.CompilerParams(vmem_limit_bytes=LIMIT),
        name="adjoint",
    )(
        diffusivity, image, slope, full.reshape(SLOTS, 8, R), lonrecv, latrecv, latmsg, cutoff.reshape(1, R), zonal,
        input_weight, output_weight, base, turn,
    )


def solution(mesh):
    placed = (
        P(None, "lon", "lat"),
        P(None, "lon", "lat"),
        P("lon", "lat"),
        P(),
        P("lat"),
        P("lat"),
        P(),
        P(),
        P(),
        P(),
    )
    return jax.shard_map(
        per_device,
        mesh=mesh,
        in_specs=placed,
        out_specs=(P(None, "lon", "lat"), P(None, "lon", "lat")),
        check_vma=False,
    )
```

```python
import functools
import math

import jax
import jax.numpy as jnp
import numpy as np
from jax import lax
from jax.experimental import pallas as pl
from jax.experimental.pallas import tpu as pltpu
from jax.sharding import PartitionSpec as P

LONGITUDE_COUNT = 5760
C = 18
HID = 48
L = 90
LP = 96
R = 128
KW = 64
N_LON = 64
N_LAT = 8
F32 = jnp.float32
BF16 = jnp.bfloat16
MESH = pl.DeviceIdType.MESH

WIDTH = [min(64, -(-(8 * a + 4) * 16 // 15)) for a in range(8)]
FOLD = []
for kind in (0, 1):
    FOLD += [((kind, 7), None), ((kind, 6), (kind, 0)), ((kind, 5), (kind, 1)), ((kind, 4), (kind, 2))]
FOLD.append(((0, 3), (1, 3)))
U_FWD, U_SPEC, U_REB, U_ADJ = 1, 3, 3, 1
PAIRS = C // 2
PER_OWNER = 3
TILES = PAIRS * len(FOLD)
OWNERS = -(-TILES // PER_OWNER)
SLOTS = OWNERS * PER_OWNER


def base_tables():
    wave = np.arange(1, KW + 1)
    rows = np.zeros((2, LP, 2 * KW), np.float64)
    for row in range(LP):
        if row <= L or row == LP - 1:
            angle = 2 * math.pi * (((row if row <= L else -1) * wave) % LONGITUDE_COUNT) / LONGITUDE_COUNT
            rows[0, row] = np.concatenate([np.cos(angle)] * 2)
            rows[1, row] = np.concatenate([np.sin(angle)] * 2)
    turn = np.zeros((N_LON, 2, 2 * KW), np.float64)
    for p in range(N_LON):
        angle = 2 * math.pi * ((p * L * wave) % LONGITUDE_COUNT) / LONGITUDE_COUNT
        turn[p, 0] = np.concatenate([np.cos(angle), np.sin(angle)])
        turn[p, 1] = np.concatenate([-np.sin(angle), np.cos(angle)])
    return rows.astype(np.float32), turn.astype(np.float32)


def iota(shape, dim):
    return lax.broadcasted_iota(jnp.int32, shape, dim)


def one_hot(mask):
    return jnp.where(mask, 1.0, 0.0).astype(BF16)


def dot(a, b):
    return lax.dot_general(a, b, (((1,), (0,)), ((), ())), preferred_element_type=F32)


def dot_nt(a, b, precision=None):
    return lax.dot_general(a, b, (((1,), (1,)), ((), ())), preferred_element_type=F32, precision=precision)


def split(x):
    high = x.astype(BF16)
    return high, (x - high.astype(F32)).astype(BF16)


def is_polar():
    lat = lax.axis_index("lat")
    return (lat == 0) | (lat == N_LAT - 1)


def polar_row(d):
    return jnp.where(lax.axis_index("lat") == N_LAT - 1, R - 1 - d, d)


def pair_select():
    row, col = iota((2 * R, R), 0), iota((2 * R, R), 1)
    return one_hot(((row >> 7) == (col >> 6)) & ((row & 127) == polar_row(col & 63)))


def pair_select_back():
    row, col = iota((R, 2 * R), 0), iota((R, 2 * R), 1)
    return one_hot(((col >> 7) == (row >> 6)) & ((col & 127) == polar_row(row & 63)))


def pack16(x):
    n = x.shape[0] * 8
    return jnp.concatenate([x[:, :8, :].reshape(n, R), x[:, 8:, :].reshape(n, R)], axis=1)


def spread_rows(n):
    return one_hot((iota((8 * n, n), 0) >> 3) == iota((8 * n, n), 1))


def spread_cols(n):
    return one_hot((iota((n, 8 * n), 1) >> 3) == iota((n, 8 * n), 0))


def diag8(x):
    return jnp.where((iota(x.shape, 0) & 7) == (iota(x.shape, 1) & 7), x, 0.0).astype(BF16)


def rows(x):
    return x.reshape(LP // 8, 8, R)


def diffusion(x, row_ref, d, lane, extra=None):
    zonal = pltpu.roll(x, 1, 0) + pltpu.roll(x, LP - 1, 0) - 2.0 * x
    east = jnp.where(lane == R - 1, 0.0, pltpu.roll(x, R - 1, 1))
    west = jnp.where(lane == 0, 0.0, pltpu.roll(x, 1, 1))
    meridional = east + west - 2.0 * x
    if extra is not None:
        meridional = meridional + extra
    return (d[None] * (row_ref[0][None] * rows(zonal) + rows(meridional))).reshape(LP, R)


def tile_of(ref, n):
    return ref[n // PER_OWNER, n % PER_OWNER]


def step_kernel(
    bg_hbm, pert_hbm, index_hbm, table_hbm, cutoff_hbm, zonal_hbm, diff_hbm, win_hbm, bias_hbm, wout_hbm, base_hbm, turn_hbm,
    tangent_ref, gradient_ref,
    image_ref, slope_ref, spec_ref, pf, d_ref, row_ref, win_ref, wout_ref, basis_ref,
    bg_ref, pert_ref, index_ref, table_ref, cutoff_ref, zonal_ref, diff_ref, bias_ref, base_ref, turn_ref,
    bf, bias_tile, a_in, a_out, mixed, sems,
    full_ref, lonrecv_ref, latrecv_ref, latmsg_ref, a_back, a_last, b_ref, back_ref, g_ref,
    parts, total, lonmsg_ref, adj, part_ref, corr, send_sem, lon_sem, lat_sem, rs_sem, ag_sem, own_sem,
):
    moves = [
        (win_hbm, win_ref), (wout_hbm, wout_ref), (bias_hbm, bias_ref), (diff_hbm, diff_ref), (table_hbm, table_ref),
        (bg_hbm, bg_ref), (pert_hbm, pert_ref), (index_hbm, index_ref), (cutoff_hbm, cutoff_ref), (zonal_hbm, zonal_ref),
        (base_hbm, base_ref), (turn_hbm.at[lax.axis_index("lon")], turn_ref),
    ]
    moves = [pltpu.make_async_copy(src, dst, sems.at[i]) for i, (src, dst) in enumerate(moves)]
    for move in moves:
        move.start()
    lat, lon = lax.axis_index("lat"), lax.axis_index("lon")
    polar = is_polar()
    owner = lon < OWNERS
    barrier = pltpu.get_barrier_semaphore()
    left, right = lax.rem(lon + N_LON - 1, N_LON), lax.rem(lon + 1, N_LON)
    around = (left, lon, right)

    def greet(lat_to, lon_to):
        pl.semaphore_signal(barrier, inc=1, device_id=(lat_to, lon_to), device_id_type=MESH)

    @pl.when(polar & owner)
    def _():
        def tell(d, carry):
            greet(lat, lax.rem(lon + d, N_LON))
            return carry

        lax.fori_loop(1, N_LON, tell, 0)

    greet(lat, left)
    greet(lat, right)

    @pl.when(lat > 0)
    def _():
        for to in around:
            greet(lat - 1, to)

    @pl.when(lat < N_LAT - 1)
    def _():
        for to in around:
            greet(lat + 1, to)

    for move in moves[:5]:
        move.wait()
    col = iota((C, 160), 1)
    cols_in = one_hot(jnp.where(col < 144, col >> 3, 0) == iota((C, 160), 0))
    a_in[...] = diag8(dot(dot_nt(spread_rows(HID), win_ref[...]).astype(BF16), cols_in))
    for i, part in enumerate(split(0.5 * wout_ref[...])):
        a_out[i] = diag8(dot(dot(spread_rows(C), part).astype(BF16), spread_cols(HID)))
    for h in range(HID):
        bias_tile[8 * h : 8 * h + 8, :] = jnp.full((8, R), bias_ref[h], F32)
    for c in range(C):
        d_ref[c] = jnp.full((8, R), diff_ref[c], F32)

    for move in moves[5:]:
        move.wait()
    surf = jnp.zeros((L, R), F32)
    index = index_ref[...]
    for s in range(16):
        surf = jnp.where(index == s, table_ref[s], surf)
    pf[:, 0:L, :] = pert_ref[...].astype(F32)
    pf[0, 0:L, :] = pert_ref[0].astype(F32) + surf
    pf[:, L:LP, :] = jnp.zeros((C, LP - L, R), F32)
    bf[:, 0:L, :] = bg_ref[...].astype(F32)
    bf[:, L:LP, :] = jnp.zeros((C, LP - L, R), F32)
    row_ref[0] = jnp.broadcast_to(zonal_ref[...], (8, R))
    row_ref[1] = jnp.broadcast_to(cutoff_ref[...].astype(F32), (8, R))
    basis_ref[...] = base_ref[0] * turn_ref[0:1, :] + base_ref[1] * turn_ref[1:2, :]

    lane = iota((LP, R), 1)

    def columns(p, carry):
        start = pl.multiple_of(p * 16, 16)
        xb = pack16(bf[:, pl.ds(start, 16), :]).astype(BF16)
        xb = jnp.concatenate([xb, jnp.zeros((16, 2 * R), BF16)], axis=0)
        pre = dot(a_in[...], xb)
        b = bias_tile[...]
        active = jnp.tanh(pre + jnp.concatenate([b, b], axis=1))
        slope = 1.0 - active * active
        slope_ref[:, pl.ds(start, 8), :] = slope[:, :R].reshape(HID, 8, R)
        slope_ref[:, pl.ds(start + 8, 8), :] = slope[:, R:].reshape(HID, 8, R)
        xp = pack16(pf[:, pl.ds(start, 16), :])
        top = xp[0:8]
        rest = top - top.astype(BF16).astype(F32)
        last = rest - rest.astype(BF16).astype(F32)
        xp = jnp.concatenate([xp, rest, last], axis=0).astype(BF16)
        high, low = split(slope * dot(a_in[...], xp))
        part = dot(a_out[0], high) + dot(a_out[0], low) + dot(a_out[1], high)
        mixed[:, pl.ds(start, 8), :] = part[:, :R].reshape(C, 8, R)
        mixed[:, pl.ds(start + 8, 8), :] = part[:, R:].reshape(C, 8, R)
        for i in range(3):
            c = 3 * p + i
            x = pf[c]
            image_ref[c] = x + diffusion(x, row_ref, d_ref[c], lane)
        return carry

    lax.fori_loop(0, LP // 16, columns, 0, unroll=U_FWD)

    @pl.when(jnp.logical_not(is_polar()))
    def _():
        image_ref[...] += mixed[...]

    @pl.when(is_polar())
    def _():
        bt = jnp.concatenate([basis_ref[...], jnp.zeros((R - LP, R), F32)], axis=0).T
        bt_high, bt_low = split(bt[:, :LP])
        select = pair_select()
        lane64 = iota((8, R), 1) & 63

        def spectra(q, carry):
            x = []
            for h in range(2):
                x.append(image_ref[2 * q + h] + mixed[2 * q + h])
                image_ref[2 * q + h] = x[h]
            high, low = split(jnp.concatenate(x, axis=1))
            high = dot(high, select).astype(BF16)
            low = dot(low, select).astype(BF16)
            s = dot(bt_high, high) + dot(bt_high, low) + dot(bt_low, high)
            for i, (big, small) in enumerate(FOLD):
                at = 64 * big[0] + 8 * big[1]
                tile = s[at : at + 8, :]
                if small is not None:
                    at = 64 * small[0] + 8 * small[1]
                    moved = pltpu.roll(s[at : at + 8, :], 64 - WIDTH[small[1]], 1)
                    tile = jnp.where(lane64 < WIDTH[big[1]], tile, moved)
                n = q * len(FOLD) + i
                spec_ref[n // PER_OWNER, n % PER_OWNER] = tile
            return carry

        lax.fori_loop(0, PAIRS, spectra, 0, unroll=U_SPEC)
        for i in range(TILES, SLOTS):
            spec_ref[i // PER_OWNER, i % PER_OWNER] = jnp.zeros((8, R), F32)

    sides = (lat > 0).astype(jnp.int32) + (lat < N_LAT - 1).astype(jnp.int32)
    owners = polar.astype(jnp.int32) * (OWNERS - owner.astype(jnp.int32))
    pl.semaphore_wait(barrier, 2 + 3 * sides + owners)

    def remote(src, dst, send, recv, lat_to, lon_to):
        return pltpu.make_async_remote_copy(
            src_ref=src, dst_ref=dst, send_sem=send, recv_sem=recv, device_id=(lat_to, lon_to), device_id_type=MESH
        )

    def wait(ref, sem):
        pltpu.make_async_copy(ref, ref, sem).wait()

    @pl.when(polar)
    def _():
        def scatter(o, carry):
            @pl.when(o != lon)
            def _():
                remote(spec_ref.at[o], parts.at[lon], send_sem.at[0], rs_sem, lat, o).start()

            return carry

        lax.fori_loop(0, OWNERS, scatter, 0)

        @pl.when(owner)
        def _():
            pltpu.make_async_copy(spec_ref.at[lon], parts.at[lon], own_sem.at[0]).start()

    row8, lane8 = iota((8, R), 0), iota((8, R), 1)
    edge = ((lane8 == 0) & (row8 < 2)) | ((lane8 == R - 1) & (row8 >= 2) & (row8 < 4))
    pick_image = jnp.where(edge & ((row8 & 1) == 0), 1.0, 0.0)
    pick_pert = jnp.where(edge & ((row8 & 1) == 1), 1.0, 0.0)
    top = lax.Precision.HIGHEST
    for c in range(C):
        x = image_ref[c]
        lonmsg_ref[0, 0, c : c + 1, :] = x[0:1, :]
        lonmsg_ref[0, 1, c : c + 1, :] = x[LP - 1 : LP, :]
        lonmsg_ref[1, 0, c : c + 1, :] = x[L - 1 : L, :]
        lonmsg_ref[1, 1, c : c + 1, :] = x[L : L + 1, :]
        cut = dot_nt(pick_image, x, top) + dot_nt(pick_pert, (d_ref[c][None] * rows(pf[c])).reshape(LP, R), top)
        for e in range(4):
            latmsg_ref[e // 2, e % 2, c : c + 1, 0:LP] = cut[e : e + 1, :]

    remote(lonmsg_ref.at[1], lonrecv_ref.at[0], send_sem.at[1], lon_sem, lat, right).start()
    remote(lonmsg_ref.at[0], lonrecv_ref.at[1], send_sem.at[1], lon_sem, lat, left).start()

    @pl.when(lat > 0)
    def _():
        for i, to in enumerate(around):
            remote(latmsg_ref.at[0], latrecv_ref.at[1, 2 - i], send_sem.at[2], lat_sem.at[1], lat - 1, to).start()

    @pl.when(lat < N_LAT - 1)
    def _():
        for i, to in enumerate(around):
            remote(latmsg_ref.at[1], latrecv_ref.at[0, 2 - i], send_sem.at[3], lat_sem.at[0], lat + 1, to).start()

    part = split(0.5 * wout_ref[...])
    col_c = spread_cols(C)
    for i in range(2):
        a_back[i] = diag8(dot(dot_nt(spread_rows(HID), part[i]).astype(BF16), col_c))
    a_last[...] = diag8(dot(dot(spread_rows(C), win_ref[...]).astype(BF16), spread_cols(HID)))

    @pl.when(polar)
    def _():
        row, col = iota((R, R), 0), iota((R, R), 1)
        pick = one_hot(row == polar_row(col & 63))
        cut = dot(row_ref[1].astype(BF16), pick)[0:1, :]
        wave = ((row & 63) + 1).astype(F32)
        ratio = cut / wave
        g = jnp.where(wave > cut, 1.0 - ratio * ratio, 0.0)
        g_ref[0] = g * (2.0 / LONGITUDE_COUNT)
        g_ref[1] = g * (2.0 - g) * (2.0 / LONGITUDE_COUNT)
        b_ref[0], b_ref[1] = split(basis_ref[...])
        back_ref[...] = pair_select_back()

    @pl.when(polar & owner)
    def _():
        wait(parts.at[pl.ds(0, N_LON - 1)], rs_sem)
        wait(parts.at[0], own_sem.at[0])

        def add(i, acc):
            return acc + parts[i]

        total[...] = lax.fori_loop(0, N_LON, add, jnp.zeros((PER_OWNER, 8, R), F32))

        def gather(d, carry):
            remote(total, full_ref.at[lon], send_sem.at[4], ag_sem, lat, lax.rem(lon + d, N_LON)).start()
            return carry

        lax.fori_loop(1, N_LON, gather, 0)
        pltpu.make_async_copy(total, full_ref.at[lon], own_sem.at[1]).start()

    wait(lonrecv_ref, lon_sem)
    wait(lonrecv_ref, send_sem.at[1])

    @pl.when(lat > 0)
    def _():
        wait(latrecv_ref.at[0], lat_sem.at[0])
        wait(latrecv_ref.at[0], send_sem.at[2])

    @pl.when(lat < N_LAT - 1)
    def _():
        wait(latrecv_ref.at[1], lat_sem.at[1])
        wait(latrecv_ref.at[1], send_sem.at[3])

    lane24 = iota((24, R), 1)
    live = iota((24, R), 0) < C

    def neighbours(side, own):
        image, pert = [[latrecv_ref[side, i, kind] for i in range(3)] for kind in range(2)]
        fix = jnp.where(lane24 < L, pert[1], 0.0)
        fix = jnp.where(lane24 == L, pltpu.roll(pert[2], L, 1), fix)
        fix = jnp.where(lane24 == LP - 1, pltpu.roll(pert[0], LP - L, 1), fix)
        halo = image[1] + own
        halo = halo + jnp.where(lane24 == 0, pltpu.roll(image[0], R - L, 1), 0.0)
        halo = halo + jnp.where(lane24 == L - 1, pltpu.roll(image[2], R - (LP - L), 1), 0.0)
        halo = jnp.where(lane24 < L, halo, 0.0)
        there = (lat > 0) if side == 0 else (lat < N_LAT - 1)
        return jnp.where(live & there, fix, 0.0), jnp.where(live & there, halo, 0.0)

    down_fix, down_halo = neighbours(0, latmsg_ref[0, 1])
    up_fix, up_halo = neighbours(1, latmsg_ref[1, 1])
    corr[...] = jnp.concatenate([down_fix, up_fix, down_halo, up_halo, jnp.zeros((32, R), F32)], axis=0).T

    lane = iota((LP, R), 1)
    row8 = iota((8, R), 0)

    def at_edges(c, first):
        low = corr[0:LP, first + c : first + c + 1]
        high = corr[0:LP, first + 24 + c : first + 25 + c]
        return jnp.where(lane == 0, low, jnp.where(lane == R - 1, high, 0.0))

    for c in range(C):
        adj[c] = image_ref[c] + at_edges(c, 0)
        adj[c, 0:8, :] += jnp.where(row8 == 0, lonrecv_ref[0, 1, c : c + 1, :], 0.0)
        end = jnp.where(row8 == 1, lonrecv_ref[1, 1, c : c + 1, :], 0.0)
        end = jnp.where(row8 == 2, lonrecv_ref[1, 0, c : c + 1, :], end)
        end = jnp.where(row8 == 7, lonrecv_ref[0, 0, c : c + 1, :], end)
        adj[c, LP - 8 : LP, :] += end

    @pl.when(polar & owner)
    def _():
        wait(full_ref.at[pl.ds(0, OWNERS - 1)], ag_sem)
        wait(total, own_sem.at[1])
        wait(parts.at[pl.ds(0, N_LON - 1)], send_sem.at[4])
        wait(full_ref.at[pl.ds(0, OWNERS - 1)], send_sem.at[0])

    @pl.when(polar & jnp.logical_not(owner))
    def _():
        wait(full_ref, ag_sem)
        wait(full_ref, send_sem.at[0])

    @pl.when(jnp.logical_not(is_polar()))
    def _():
        tangent_ref[...] = adj[:, 0:L, :].astype(BF16)

    @pl.when(is_polar())
    def _():
        g_tangent, g_adjoint = g_ref[0], g_ref[1]
        b_high, b_low = b_ref[0], b_ref[1]
        back = back_ref[...]

        def rebuild(q, carry):
            tiles = {}
            for i, (big, small) in enumerate(FOLD):
                tile = tile_of(full_ref, q * len(FOLD) + i)
                tiles[big] = tile
                if small is not None:
                    tiles[small] = pltpu.roll(tile, R - 64 + WIDTH[small[1]], 1)
            s = jnp.concatenate([tiles[kind, a] for kind in (0, 1) for a in range(8)], axis=0)
            high, low = split(jnp.concatenate([g_tangent * s, g_adjoint * s], axis=1))
            removed = dot(b_high, high) + dot(b_high, low) + dot(b_low, high)
            removed = jnp.concatenate([removed[:, :R], removed[:, R:]], axis=0)
            high, low = split(removed)
            removed = dot(high, back) + dot(low, back)
            for h in range(2):
                c = 2 * q + h
                x = adj[c]
                lanes = slice(h * R, (h + 1) * R)
                tangent_ref[c] = (x - removed[:LP, lanes])[0:L].astype(BF16)
                adj[c] = x - removed[LP:, lanes]
            return carry

        lax.fori_loop(0, PAIRS, rebuild, 0, unroll=U_REB)

    def columns_back(p, carry):
        start = pl.multiple_of(p * 16, 16)
        high, low = split(pack16(adj[:, pl.ds(start, 16), :]))
        hidden = dot(a_back[0], high) + dot(a_back[0], low) + dot(a_back[1], high)
        high, low = split(hidden * pack16(slope_ref[:, pl.ds(start, 16), :]))
        part = dot(a_last[...], high) + dot(a_last[...], low)
        part_ref[:, pl.ds(start, 8), :] = part[:, :R].reshape(C, 8, R)
        part_ref[:, pl.ds(start + 8, 8), :] = part[:, R:].reshape(C, 8, R)
        return carry

    lax.fori_loop(0, LP // 16, columns_back, 0, unroll=U_ADJ)

    for c in range(C):
        x = adj[c]
        out = x + diffusion(x, row_ref, d_ref[c], lane, at_edges(c, 48)) + part_ref[c]
        gradient_ref[c] = out[0:L].astype(BF16)


def vmem():
    return pl.BlockSpec(memory_space=pltpu.VMEM)


def hbm():
    return pl.BlockSpec(memory_space=pltpu.HBM)


def anywhere():
    return pl.BlockSpec(memory_space=pl.ANY)


LIMIT = 58 * 2**20


def per_device(
    background_state,
    perturbation,
    surface_pattern_index,
    surface_amplitude_table,
    cutoff,
    zonal_row_weight,
    diffusivity,
    input_weight,
    bias,
    output_weight,
):
    base, turn = (jnp.asarray(t) for t in base_tables())
    shape = jax.ShapeDtypeStruct
    scratch = pltpu.VMEM
    field = scratch((C, LP, R), F32)
    message = scratch((2, 2, 24, R), F32)
    dma = pltpu.SemaphoreType.DMA
    return pl.pallas_call(
        step_kernel,
        out_shape=(shape((C, L, R), BF16), shape((C, L, R), BF16)),
        in_specs=[hbm()] * 12,
        out_specs=(vmem(), vmem()),
        scratch_shapes=[
            field,
            scratch((HID, LP, R), F32),
            scratch((OWNERS, PER_OWNER, 8, R), F32),
            field,
            scratch((C, 8, R), F32),
            scratch((2, 8, R), F32),
            scratch((C, HID), BF16),
            scratch((C, HID), F32),
            scratch((LP, R), F32),
            scratch((C, L, R), BF16),
            scratch((C, L, R), BF16),
            scratch((L, R), jnp.int32),
            pltpu.SMEM((16,), F32),
            scratch((1, R), jnp.int32),
            scratch((1, R), F32),
            pltpu.SMEM((C,), F32),
            pltpu.SMEM((HID,), F32),
            scratch((2, LP, R), F32),
            scratch((2, R), F32),
            field,
            scratch((8 * HID, R), F32),
            scratch((8 * HID, 160), BF16),
            scratch((2, 8 * C, 8 * HID), BF16),
            field,
            dma((12,)),
            scratch((OWNERS, PER_OWNER, 8, R), F32),
            message,
            scratch((2, 3, 2, 24, R), F32),
            message,
            scratch((2, 8 * HID, 8 * C), BF16),
            scratch((8 * C, 8 * HID), BF16),
            scratch((2, LP, R), BF16),
            scratch((R, 2 * R), BF16),
            scratch((2, R, R), F32),
            scratch((N_LON, PER_OWNER, 8, R), F32),
            scratch((PER_OWNER, 8, R), F32),
            message,
            field,
            field,
            scratch((R, R), F32),
            dma((5,)),
            dma,
            dma((2,)),
            dma,
            dma,
            dma((2,)),
        ],
        compiler_params=pltpu.CompilerParams(collective_id=0, has_side_effects=True, vmem_limit_bytes=LIMIT),
        name="step",
    )(
        background_state, perturbation, surface_pattern_index, surface_amplitude_table, cutoff.reshape(1, R),
        zonal_row_weight.reshape(1, R), diffusivity, input_weight.T, bias, output_weight, base, turn,
    )


def solution(mesh):
    placed = (
        P(None, "lon", "lat"),
        P(None, "lon", "lat"),
        P("lon", "lat"),
        P(),
        P("lat"),
        P("lat"),
        P(),
        P(),
        P(),
        P(),
    )
    return jax.shard_map(
        per_device,
        mesh=mesh,
        in_specs=placed,
        out_specs=(P(None, "lon", "lat"), P(None, "lon", "lat")),
        check_vma=False,
    )
```

```python
import functools
import math

import jax
import jax.numpy as jnp
import numpy as np
from jax import lax
from jax.experimental import pallas as pl
from jax.experimental.pallas import tpu as pltpu
from jax.sharding import PartitionSpec as P

LONGITUDE_COUNT = 5760
C = 18
HID = 48
L = 90
LP = 96
R = 128
KW = 64
N_LON = 64
N_LAT = 8
PLANE = 32
F32 = jnp.float32
BF16 = jnp.bfloat16
MESH = pl.DeviceIdType.MESH

WIDTH = [min(64, -(-(8 * a + 4) * 16 // 15)) for a in range(8)]
FOLD = []
for kind in (0, 1):
    FOLD += [((kind, 7), None), ((kind, 6), (kind, 0)), ((kind, 5), (kind, 1)), ((kind, 4), (kind, 2))]
FOLD.append(((0, 3), (1, 3)))
U_FWD, U_SPEC, U_REB, U_ADJ = 3, 9, 9, 6
PAIRS = C // 2
PER_OWNER = 3
TILES = PAIRS * len(FOLD)
OWNERS = -(-TILES // PER_OWNER)
SLOTS = OWNERS * PER_OWNER


def base_tables():
    wave = np.arange(1, KW + 1)
    rows = np.zeros((2, LP, 2 * KW), np.float64)
    for row in range(LP):
        if row <= L or row == LP - 1:
            angle = 2 * math.pi * (((row if row <= L else -1) * wave) % LONGITUDE_COUNT) / LONGITUDE_COUNT
            rows[0, row] = np.concatenate([np.cos(angle)] * 2)
            rows[1, row] = np.concatenate([np.sin(angle)] * 2)
    turn = np.zeros((N_LON, 2, 2 * KW), np.float64)
    for p in range(N_LON):
        angle = 2 * math.pi * ((p * L * wave) % LONGITUDE_COUNT) / LONGITUDE_COUNT
        turn[p, 0] = np.concatenate([np.cos(angle), np.sin(angle)])
        turn[p, 1] = np.concatenate([-np.sin(angle), np.cos(angle)])
    return rows.astype(np.float32), turn.astype(np.float32)


def iota(shape, dim):
    return lax.broadcasted_iota(jnp.int32, shape, dim)


def one_hot(mask):
    return jnp.where(mask, 1.0, 0.0).astype(BF16)


def dot(a, b):
    return lax.dot_general(a, b, (((1,), (0,)), ((), ())), preferred_element_type=F32)


def dot_nt(a, b, precision=None):
    return lax.dot_general(a, b, (((1,), (1,)), ((), ())), preferred_element_type=F32, precision=precision)


def split(x):
    high = x.astype(BF16)
    return high, (x - high.astype(F32)).astype(BF16)


def is_polar():
    lat = lax.axis_index("lat")
    return (lat == 0) | (lat == N_LAT - 1)


def polar_row(d):
    return jnp.where(lax.axis_index("lat") == N_LAT - 1, R - 1 - d, d)


def pair_select():
    row, col = iota((2 * R, R), 0), iota((2 * R, R), 1)
    return one_hot(((row >> 7) == (col >> 6)) & ((row & 127) == polar_row(col & 63)))


def pair_select_back():
    row, col = iota((R, 2 * R), 0), iota((R, 2 * R), 1)
    return one_hot(((col >> 7) == (row >> 6)) & ((col & 127) == polar_row(row & 63)))


def pack16(x):
    n = x.shape[0] * 8
    return jnp.concatenate([x[:, :8, :].reshape(n, R), x[:, 8:, :].reshape(n, R)], axis=1)


def spread_rows(n):
    return one_hot((iota((8 * n, n), 0) >> 3) == iota((8 * n, n), 1))


def spread_cols(n):
    return one_hot((iota((n, 8 * n), 1) >> 3) == iota((n, 8 * n), 0))


def diag8(x):
    return jnp.where((iota(x.shape, 0) & 7) == (iota(x.shape, 1) & 7), x, 0.0).astype(BF16)


def rows(x):
    return x.reshape(LP // 8, 8, R)


def diffusion(x, row_ref, d, lane, extra=None):
    zonal = pltpu.roll(x, 1, 0) + pltpu.roll(x, LP - 1, 0) - 2.0 * x
    east = jnp.where(lane == R - 1, 0.0, pltpu.roll(x, R - 1, 1))
    west = jnp.where(lane == 0, 0.0, pltpu.roll(x, 1, 1))
    meridional = east + west - 2.0 * x
    if extra is not None:
        meridional = meridional + extra
    return (d[None] * (row_ref[0][None] * rows(zonal) + rows(meridional))).reshape(LP, R)


def tile_of(ref, n):
    return ref[n // PER_OWNER, n % PER_OWNER]


def step_kernel(
    bg_hbm, pert_hbm, index_hbm, table_hbm, cutoff_hbm, zonal_hbm, diff_hbm, win_hbm, bias_hbm, wout_hbm, base_hbm, turn_hbm,
    tangent_ref, gradient_ref,
    image_ref, slope_ref, spec_ref, pf, d_ref, row_ref, win_ref, wout_ref, basis_ref,
    bg_ref, pert_ref, index_ref, table_ref, cutoff_ref, zonal_ref, diff_ref, bias_ref, base_ref, turn_ref,
    bf, bias_tile, a_in, a_out, mixed, sems,
    full_ref, lonrecv_ref, latrecv_ref, latmsg_ref, a_back, a_last, b_ref, back_ref, g_ref,
    parts, total, lonmsg_ref, adj, part_ref, corr, send_sem, lon_sem, lat_sem, rs_sem, ag_sem, own_sem, pair_sem,
):
    moves = [
        (win_hbm, win_ref), (wout_hbm, wout_ref), (bias_hbm, bias_ref), (diff_hbm, diff_ref), (table_hbm, table_ref),
        (bg_hbm, bg_ref), (pert_hbm, pert_ref), (index_hbm, index_ref), (cutoff_hbm, cutoff_ref), (zonal_hbm, zonal_ref),
        (base_hbm, base_ref), (turn_hbm.at[lax.axis_index("lon")], turn_ref),
    ]
    moves = [pltpu.make_async_copy(src, dst, sems.at[i]) for i, (src, dst) in enumerate(moves)]
    for move in moves:
        move.start()
    lat, lon = lax.axis_index("lat"), lax.axis_index("lon")
    polar = is_polar()
    here = lax.rem(lon, PLANE)
    first = lon - here
    owner = here < OWNERS
    partner = lax.rem(lon + PLANE, N_LON)
    barrier = pltpu.get_barrier_semaphore()
    left, right = lax.rem(lon + N_LON - 1, N_LON), lax.rem(lon + 1, N_LON)
    around = (left, lon, right)

    def greet(lat_to, lon_to):
        pl.semaphore_signal(barrier, inc=1, device_id=(lat_to, lon_to), device_id_type=MESH)

    @pl.when(polar & owner)
    def _():
        def tell(d, carry):
            greet(lat, first + lax.rem(here + d, PLANE))
            return carry

        lax.fori_loop(1, PLANE, tell, 0)
        greet(lat, partner)

    greet(lat, left)
    greet(lat, right)

    @pl.when(lat > 0)
    def _():
        for to in around:
            greet(lat - 1, to)

    @pl.when(lat < N_LAT - 1)
    def _():
        for to in around:
            greet(lat + 1, to)

    for move in moves[:5]:
        move.wait()
    col = iota((C, 160), 1)
    cols_in = one_hot(jnp.where(col < 144, col >> 3, 0) == iota((C, 160), 0))
    a_in[...] = diag8(dot(dot_nt(spread_rows(HID), win_ref[...]).astype(BF16), cols_in))
    for i, part in enumerate(split(0.5 * wout_ref[...])):
        a_out[i] = diag8(dot(dot(spread_rows(C), part).astype(BF16), spread_cols(HID)))
    for h in range(HID):
        bias_tile[8 * h : 8 * h + 8, :] = jnp.full((8, R), bias_ref[h], F32)
    for c in range(C):
        d_ref[c] = jnp.full((8, R), diff_ref[c], F32)

    for move in moves[5:]:
        move.wait()
    surf = jnp.zeros((L, R), F32)
    index = index_ref[...]
    for s in range(16):
        surf = jnp.where(index == s, table_ref[s], surf)
    pf[:, 0:L, :] = pert_ref[...].astype(F32)
    pf[0, 0:L, :] = pert_ref[0].astype(F32) + surf
    pf[:, L:LP, :] = jnp.zeros((C, LP - L, R), F32)
    bf[:, 0:L, :] = bg_ref[...].astype(F32)
    bf[:, L:LP, :] = jnp.zeros((C, LP - L, R), F32)
    row_ref[0] = jnp.broadcast_to(zonal_ref[...], (8, R))
    row_ref[1] = jnp.broadcast_to(cutoff_ref[...].astype(F32), (8, R))
    basis_ref[...] = base_ref[0] * turn_ref[0:1, :] + base_ref[1] * turn_ref[1:2, :]

    lane = iota((LP, R), 1)

    def columns(p, carry):
        start = pl.multiple_of(p * 16, 16)
        xb = pack16(bf[:, pl.ds(start, 16), :]).astype(BF16)
        xb = jnp.concatenate([xb, jnp.zeros((16, 2 * R), BF16)], axis=0)
        pre = dot(a_in[...], xb)
        b = bias_tile[...]
        active = jnp.tanh(pre + jnp.concatenate([b, b], axis=1))
        slope = 1.0 - active * active
        slope_ref[:, pl.ds(start, 8), :] = slope[:, :R].reshape(HID, 8, R)
        slope_ref[:, pl.ds(start + 8, 8), :] = slope[:, R:].reshape(HID, 8, R)
        xp = pack16(pf[:, pl.ds(start, 16), :])
        top = xp[0:8]
        rest = top - top.astype(BF16).astype(F32)
        last = rest - rest.astype(BF16).astype(F32)
        xp = jnp.concatenate([xp, rest, last], axis=0).astype(BF16)
        high, low = split(slope * dot(a_in[...], xp))
        part = dot(a_out[0], high) + dot(a_out[0], low) + dot(a_out[1], high)
        mixed[:, pl.ds(start, 8), :] = part[:, :R].reshape(C, 8, R)
        mixed[:, pl.ds(start + 8, 8), :] = part[:, R:].reshape(C, 8, R)
        for i in range(3):
            c = 3 * p + i
            x = pf[c]
            image_ref[c] = x + diffusion(x, row_ref, d_ref[c], lane)
        return carry

    lax.fori_loop(0, LP // 16, columns, 0, unroll=U_FWD)

    @pl.when(jnp.logical_not(is_polar()))
    def _():
        image_ref[...] += mixed[...]

    @pl.when(is_polar())
    def _():
        bt = jnp.concatenate([basis_ref[...], jnp.zeros((R - LP, R), F32)], axis=0).T
        bt_high, bt_low = split(bt[:, :LP])
        select = pair_select()
        lane64 = iota((8, R), 1) & 63

        def spectra(q, carry):
            x = []
            for h in range(2):
                x.append(image_ref[2 * q + h] + mixed[2 * q + h])
                image_ref[2 * q + h] = x[h]
            high, low = split(jnp.concatenate(x, axis=1))
            high = dot(high, select).astype(BF16)
            low = dot(low, select).astype(BF16)
            s = dot(bt_high, high) + dot(bt_high, low) + dot(bt_low, high)
            for i, (big, small) in enumerate(FOLD):
                at = 64 * big[0] + 8 * big[1]
                tile = s[at : at + 8, :]
                if small is not None:
                    at = 64 * small[0] + 8 * small[1]
                    moved = pltpu.roll(s[at : at + 8, :], 64 - WIDTH[small[1]], 1)
                    tile = jnp.where(lane64 < WIDTH[big[1]], tile, moved)
                n = q * len(FOLD) + i
                spec_ref[n // PER_OWNER, n % PER_OWNER] = tile
            return carry

        lax.fori_loop(0, PAIRS, spectra, 0, unroll=U_SPEC)
        for i in range(TILES, SLOTS):
            spec_ref[i // PER_OWNER, i % PER_OWNER] = jnp.zeros((8, R), F32)

    sides = (lat > 0).astype(jnp.int32) + (lat < N_LAT - 1).astype(jnp.int32)
    owners = polar.astype(jnp.int32) * OWNERS
    pl.semaphore_wait(barrier, 2 + 3 * sides + owners)

    def remote(src, dst, send, recv, lat_to, lon_to):
        return pltpu.make_async_remote_copy(
            src_ref=src, dst_ref=dst, send_sem=send, recv_sem=recv, device_id=(lat_to, lon_to), device_id_type=MESH
        )

    def wait(ref, sem):
        pltpu.make_async_copy(ref, ref, sem).wait()

    @pl.when(polar)
    def _():
        def scatter(o, carry):
            @pl.when(o != here)
            def _():
                remote(spec_ref.at[o], parts.at[here], send_sem.at[0], rs_sem, lat, first + o).start()

            return carry

        lax.fori_loop(0, OWNERS, scatter, 0)

        @pl.when(owner)
        def _():
            pltpu.make_async_copy(spec_ref.at[here], parts.at[here], own_sem.at[0]).start()

    row8, lane8 = iota((8, R), 0), iota((8, R), 1)
    edge = ((lane8 == 0) & (row8 < 2)) | ((lane8 == R - 1) & (row8 >= 2) & (row8 < 4))
    pick_image = jnp.where(edge & ((row8 & 1) == 0), 1.0, 0.0)
    pick_pert = jnp.where(edge & ((row8 & 1) == 1), 1.0, 0.0)
    top = lax.Precision.HIGHEST
    for c in range(C):
        x = image_ref[c]
        lonmsg_ref[0, 0, c : c + 1, :] = x[0:1, :]
        lonmsg_ref[0, 1, c : c + 1, :] = x[LP - 1 : LP, :]
        lonmsg_ref[1, 0, c : c + 1, :] = x[L - 1 : L, :]
        lonmsg_ref[1, 1, c : c + 1, :] = x[L : L + 1, :]
        cut = dot_nt(pick_image, x, top) + dot_nt(pick_pert, (d_ref[c][None] * rows(pf[c])).reshape(LP, R), top)
        for e in range(4):
            latmsg_ref[e // 2, e % 2, c : c + 1, 0:LP] = cut[e : e + 1, :]

    remote(lonmsg_ref.at[1], lonrecv_ref.at[0], send_sem.at[1], lon_sem, lat, right).start()
    remote(lonmsg_ref.at[0], lonrecv_ref.at[1], send_sem.at[1], lon_sem, lat, left).start()

    @pl.when(lat > 0)
    def _():
        for i, to in enumerate(around):
            remote(latmsg_ref.at[0], latrecv_ref.at[1, 2 - i], send_sem.at[2], lat_sem.at[1], lat - 1, to).start()

    @pl.when(lat < N_LAT - 1)
    def _():
        for i, to in enumerate(around):
            remote(latmsg_ref.at[1], latrecv_ref.at[0, 2 - i], send_sem.at[3], lat_sem.at[0], lat + 1, to).start()

    part = split(0.5 * wout_ref[...])
    col_c = spread_cols(C)
    for i in range(2):
        a_back[i] = diag8(dot(dot_nt(spread_rows(HID), part[i]).astype(BF16), col_c))
    a_last[...] = diag8(dot(dot(spread_rows(C), win_ref[...]).astype(BF16), spread_cols(HID)))

    @pl.when(polar)
    def _():
        row, col = iota((R, R), 0), iota((R, R), 1)
        pick = one_hot(row == polar_row(col & 63))
        cut = dot(row_ref[1].astype(BF16), pick)[0:1, :]
        wave = ((row & 63) + 1).astype(F32)
        ratio = cut / wave
        g = jnp.where(wave > cut, 1.0 - ratio * ratio, 0.0)
        g_ref[0] = g * (2.0 / LONGITUDE_COUNT)
        g_ref[1] = g * (2.0 - g) * (2.0 / LONGITUDE_COUNT)
        b_ref[0], b_ref[1] = split(basis_ref[...])
        back_ref[...] = pair_select_back()

    @pl.when(polar & owner)
    def _():
        wait(parts.at[pl.ds(0, PLANE - 1)], rs_sem)
        wait(parts.at[0], own_sem.at[0])

        def add(i, acc):
            return acc + parts[i]

        total[0] = lax.fori_loop(1, PLANE, add, parts[0], unroll=True)
        remote(total.at[0], total.at[1], send_sem.at[5], pair_sem, lat, partner).start()
        wait(total.at[1], pair_sem)
        total[2] = total[0] + total[1]

        def gather(d, carry):
            to = first + lax.rem(here + d, PLANE)
            remote(total.at[2], full_ref.at[here], send_sem.at[4], ag_sem, lat, to).start()
            return carry

        lax.fori_loop(1, PLANE, gather, 0)
        pltpu.make_async_copy(total.at[2], full_ref.at[here], own_sem.at[1]).start()

    wait(lonrecv_ref, lon_sem)
    wait(lonrecv_ref, send_sem.at[1])

    @pl.when(lat > 0)
    def _():
        wait(latrecv_ref.at[0], lat_sem.at[0])
        wait(latrecv_ref.at[0], send_sem.at[2])

    @pl.when(lat < N_LAT - 1)
    def _():
        wait(latrecv_ref.at[1], lat_sem.at[1])
        wait(latrecv_ref.at[1], send_sem.at[3])

    lane24 = iota((24, R), 1)
    live = iota((24, R), 0) < C

    def neighbours(side, own):
        image, pert = [[latrecv_ref[side, i, kind] for i in range(3)] for kind in range(2)]
        fix = jnp.where(lane24 < L, pert[1], 0.0)
        fix = jnp.where(lane24 == L, pltpu.roll(pert[2], L, 1), fix)
        fix = jnp.where(lane24 == LP - 1, pltpu.roll(pert[0], LP - L, 1), fix)
        halo = image[1] + own
        halo = halo + jnp.where(lane24 == 0, pltpu.roll(image[0], R - L, 1), 0.0)
        halo = halo + jnp.where(lane24 == L - 1, pltpu.roll(image[2], R - (LP - L), 1), 0.0)
        halo = jnp.where(lane24 < L, halo, 0.0)
        there = (lat > 0) if side == 0 else (lat < N_LAT - 1)
        return jnp.where(live & there, fix, 0.0), jnp.where(live & there, halo, 0.0)

    down_fix, down_halo = neighbours(0, latmsg_ref[0, 1])
    up_fix, up_halo = neighbours(1, latmsg_ref[1, 1])
    corr[...] = jnp.concatenate([down_fix, up_fix, down_halo, up_halo, jnp.zeros((32, R), F32)], axis=0).T

    lane = iota((LP, R), 1)
    row8 = iota((8, R), 0)

    def at_edges(c, first):
        low = corr[0:LP, first + c : first + c + 1]
        high = corr[0:LP, first + 24 + c : first + 25 + c]
        return jnp.where(lane == 0, low, jnp.where(lane == R - 1, high, 0.0))

    for c in range(C):
        adj[c] = image_ref[c] + at_edges(c, 0)
        adj[c, 0:8, :] += jnp.where(row8 == 0, lonrecv_ref[0, 1, c : c + 1, :], 0.0)
        end = jnp.where(row8 == 1, lonrecv_ref[1, 1, c : c + 1, :], 0.0)
        end = jnp.where(row8 == 2, lonrecv_ref[1, 0, c : c + 1, :], end)
        end = jnp.where(row8 == 7, lonrecv_ref[0, 0, c : c + 1, :], end)
        adj[c, LP - 8 : LP, :] += end

    @pl.when(polar & owner)
    def _():
        wait(full_ref.at[pl.ds(0, OWNERS - 1)], ag_sem)
        wait(total.at[2], own_sem.at[1])
        wait(total.at[0], send_sem.at[5])
        wait(parts.at[pl.ds(0, PLANE - 1)], send_sem.at[4])
        wait(full_ref.at[pl.ds(0, OWNERS - 1)], send_sem.at[0])

    @pl.when(polar & jnp.logical_not(owner))
    def _():
        wait(full_ref, ag_sem)
        wait(full_ref, send_sem.at[0])

    @pl.when(jnp.logical_not(is_polar()))
    def _():
        tangent_ref[...] = adj[:, 0:L, :].astype(BF16)

    @pl.when(is_polar())
    def _():
        g_tangent, g_adjoint = g_ref[0], g_ref[1]
        b_high, b_low = b_ref[0], b_ref[1]
        back = back_ref[...]

        def rebuild(q, carry):
            tiles = {}
            for i, (big, small) in enumerate(FOLD):
                tile = tile_of(full_ref, q * len(FOLD) + i)
                tiles[big] = tile
                if small is not None:
                    tiles[small] = pltpu.roll(tile, R - 64 + WIDTH[small[1]], 1)
            s = jnp.concatenate([tiles[kind, a] for kind in (0, 1) for a in range(8)], axis=0)
            high, low = split(jnp.concatenate([g_tangent * s, g_adjoint * s], axis=1))
            removed = dot(b_high, high) + dot(b_high, low) + dot(b_low, high)
            removed = jnp.concatenate([removed[:, :R], removed[:, R:]], axis=0)
            high, low = split(removed)
            removed = dot(high, back) + dot(low, back)
            for h in range(2):
                c = 2 * q + h
                x = adj[c]
                lanes = slice(h * R, (h + 1) * R)
                tangent_ref[c] = (x - removed[:LP, lanes])[0:L].astype(BF16)
                adj[c] = x - removed[LP:, lanes]
            return carry

        lax.fori_loop(0, PAIRS, rebuild, 0, unroll=U_REB)

    def columns_back(p, carry):
        start = pl.multiple_of(p * 16, 16)
        high, low = split(pack16(adj[:, pl.ds(start, 16), :]))
        hidden = dot(a_back[0], high) + dot(a_back[0], low) + dot(a_back[1], high)
        high, low = split(hidden * pack16(slope_ref[:, pl.ds(start, 16), :]))
        part = dot(a_last[...], high) + dot(a_last[...], low)
        part_ref[:, pl.ds(start, 8), :] = part[:, :R].reshape(C, 8, R)
        part_ref[:, pl.ds(start + 8, 8), :] = part[:, R:].reshape(C, 8, R)
        return carry

    lax.fori_loop(0, LP // 16, columns_back, 0, unroll=U_ADJ)

    for c in range(C):
        x = adj[c]
        out = x + diffusion(x, row_ref, d_ref[c], lane, at_edges(c, 48)) + part_ref[c]
        gradient_ref[c] = out[0:L].astype(BF16)


def vmem():
    return pl.BlockSpec(memory_space=pltpu.VMEM)


def hbm():
    return pl.BlockSpec(memory_space=pltpu.HBM)


def anywhere():
    return pl.BlockSpec(memory_space=pl.ANY)


LIMIT = 58 * 2**20


def per_device(
    background_state,
    perturbation,
    surface_pattern_index,
    surface_amplitude_table,
    cutoff,
    zonal_row_weight,
    diffusivity,
    input_weight,
    bias,
    output_weight,
):
    base, turn = (jnp.asarray(t) for t in base_tables())
    shape = jax.ShapeDtypeStruct
    scratch = pltpu.VMEM
    field = scratch((C, LP, R), F32)
    message = scratch((2, 2, 24, R), F32)
    dma = pltpu.SemaphoreType.DMA
    return pl.pallas_call(
        step_kernel,
        out_shape=(shape((C, L, R), BF16), shape((C, L, R), BF16)),
        in_specs=[hbm()] * 12,
        out_specs=(vmem(), vmem()),
        scratch_shapes=[
            field,
            scratch((HID, LP, R), F32),
            scratch((OWNERS, PER_OWNER, 8, R), F32),
            field,
            scratch((C, 8, R), F32),
            scratch((2, 8, R), F32),
            scratch((C, HID), BF16),
            scratch((C, HID), F32),
            scratch((LP, R), F32),
            scratch((C, L, R), BF16),
            scratch((C, L, R), BF16),
            scratch((L, R), jnp.int32),
            pltpu.SMEM((16,), F32),
            scratch((1, R), jnp.int32),
            scratch((1, R), F32),
            pltpu.SMEM((C,), F32),
            pltpu.SMEM((HID,), F32),
            scratch((2, LP, R), F32),
            scratch((2, R), F32),
            field,
            scratch((8 * HID, R), F32),
            scratch((8 * HID, 160), BF16),
            scratch((2, 8 * C, 8 * HID), BF16),
            field,
            dma((12,)),
            scratch((OWNERS, PER_OWNER, 8, R), F32),
            message,
            scratch((2, 3, 2, 24, R), F32),
            message,
            scratch((2, 8 * HID, 8 * C), BF16),
            scratch((8 * C, 8 * HID), BF16),
            scratch((2, LP, R), BF16),
            scratch((R, 2 * R), BF16),
            scratch((2, R, R), F32),
            scratch((PLANE, PER_OWNER, 8, R), F32),
            scratch((3, PER_OWNER, 8, R), F32),
            message,
            field,
            field,
            scratch((R, R), F32),
            dma((6,)),
            dma,
            dma((2,)),
            dma,
            dma,
            dma((2,)),
            dma,
        ],
        compiler_params=pltpu.CompilerParams(collective_id=0, has_side_effects=True, vmem_limit_bytes=LIMIT),
        name="step",
    )(
        background_state, perturbation, surface_pattern_index, surface_amplitude_table, cutoff.reshape(1, R),
        zonal_row_weight.reshape(1, R), diffusivity, input_weight.T, bias, output_weight, base, turn,
    )


def solution(mesh):
    placed = (
        P(None, "lon", "lat"),
        P(None, "lon", "lat"),
        P("lon", "lat"),
        P(),
        P("lat"),
        P("lat"),
        P(),
        P(),
        P(),
        P(),
    )
    return jax.shard_map(
        per_device,
        mesh=mesh,
        in_specs=placed,
        out_specs=(P(None, "lon", "lat"), P(None, "lon", "lat")),
        check_vma=False,
    )
```

```python
import functools
import math

import jax
import jax.numpy as jnp
import numpy as np
from jax import lax
from jax.experimental import pallas as pl
from jax.experimental.pallas import tpu as pltpu
from jax.sharding import PartitionSpec as P

LONGITUDE_COUNT = 5760
C = 18
HID = 48
L = 90
LP = 96
R = 128
KW = 64
N_LON = 64
N_LAT = 8
PLANE = 32
F32 = jnp.float32
BF16 = jnp.bfloat16
MESH = pl.DeviceIdType.MESH

WIDTH = [min(64, -(-(8 * a + 4) * 16 // 15)) for a in range(8)]
FOLD = []
for kind in (0, 1):
    FOLD += [((kind, 7), None), ((kind, 6), (kind, 0)), ((kind, 5), (kind, 1)), ((kind, 4), (kind, 2))]
FOLD.append(((0, 3), (1, 3)))
U_FWD, U_SPEC, U_REB, U_ADJ = 3, 9, 9, 3
PAIRS = C // 2
PER_OWNER = 3
TILES = PAIRS * len(FOLD)
OWNERS = -(-TILES // PER_OWNER)
SLOTS = OWNERS * PER_OWNER


def base_tables():
    wave = np.arange(1, KW + 1)
    rows = np.zeros((2, LP, 2 * KW), np.float64)
    for row in range(LP):
        if row <= L or row == LP - 1:
            angle = 2 * math.pi * (((row if row <= L else -1) * wave) % LONGITUDE_COUNT) / LONGITUDE_COUNT
            rows[0, row] = np.concatenate([np.cos(angle)] * 2)
            rows[1, row] = np.concatenate([np.sin(angle)] * 2)
    turn = np.zeros((N_LON, 2, 2 * KW), np.float64)
    for p in range(N_LON):
        angle = 2 * math.pi * ((p * L * wave) % LONGITUDE_COUNT) / LONGITUDE_COUNT
        turn[p, 0] = np.concatenate([np.cos(angle), np.sin(angle)])
        turn[p, 1] = np.concatenate([-np.sin(angle), np.cos(angle)])
    return rows.astype(np.float32), turn.astype(np.float32)


def iota(shape, dim):
    return lax.broadcasted_iota(jnp.int32, shape, dim)


def one_hot(mask):
    return jnp.where(mask, 1.0, 0.0).astype(BF16)


def dot(a, b):
    return lax.dot_general(a, b, (((1,), (0,)), ((), ())), preferred_element_type=F32)


def dot_nt(a, b, precision=None):
    return lax.dot_general(a, b, (((1,), (1,)), ((), ())), preferred_element_type=F32, precision=precision)


def split(x):
    high = x.astype(BF16)
    return high, (x - high.astype(F32)).astype(BF16)


def is_polar():
    lat = lax.axis_index("lat")
    return (lat == 0) | (lat == N_LAT - 1)


def polar_row(d):
    return jnp.where(lax.axis_index("lat") == N_LAT - 1, R - 1 - d, d)


def pair_select():
    row, col = iota((2 * R, R), 0), iota((2 * R, R), 1)
    return one_hot(((row >> 7) == (col >> 6)) & ((row & 127) == polar_row(col & 63)))


def pair_select_back():
    row, col = iota((R, 2 * R), 0), iota((R, 2 * R), 1)
    return one_hot(((col >> 7) == (row >> 6)) & ((col & 127) == polar_row(row & 63)))


def pack16(x):
    n = x.shape[0] * 8
    return jnp.concatenate([x[:, :8, :].reshape(n, R), x[:, 8:, :].reshape(n, R)], axis=1)


def spread_rows(n):
    return one_hot((iota((8 * n, n), 0) >> 3) == iota((8 * n, n), 1))


def spread_cols(n):
    return one_hot((iota((n, 8 * n), 1) >> 3) == iota((n, 8 * n), 0))


def diag8(x):
    return jnp.where((iota(x.shape, 0) & 7) == (iota(x.shape, 1) & 7), x, 0.0).astype(BF16)


def rows(x):
    return x.reshape(LP // 8, 8, R)


def diffusion(x, row_ref, d, lane, extra=None):
    zonal = pltpu.roll(x, 1, 0) + pltpu.roll(x, LP - 1, 0) - 2.0 * x
    east = jnp.where(lane == R - 1, 0.0, pltpu.roll(x, R - 1, 1))
    west = jnp.where(lane == 0, 0.0, pltpu.roll(x, 1, 1))
    meridional = east + west - 2.0 * x
    if extra is not None:
        meridional = meridional + extra
    return (d[None] * (row_ref[0][None] * rows(zonal) + rows(meridional))).reshape(LP, R)


def tile_of(ref, n):
    return ref[n // PER_OWNER, n % PER_OWNER]


def step_kernel(
    bg_hbm, pert_hbm, index_hbm, table_hbm, cutoff_hbm, zonal_hbm, diff_hbm, win_hbm, bias_hbm, wout_hbm, base_hbm, turn_hbm,
    tangent_hbm, gradient_hbm,
    tangent_ref, gradient_ref, out_sems,
    image_ref, slope_ref, spec_ref, pf, d_ref, row_ref, win_ref, wout_ref, basis_ref,
    bg_ref, pert_ref, index_ref, table_ref, cutoff_ref, zonal_ref, diff_ref, bias_ref, base_ref, turn_ref,
    bf, bias_tile, a_in, a_out, mixed, sems,
    full_ref, lonrecv_ref, latrecv_ref, latmsg_ref, a_back, a_last, b_ref, back_ref, g_ref,
    parts, total, lonmsg_ref, adj, part_ref, corr, send_sem, lon_sem, lat_sem, rs_sem, ag_sem, own_sem, pair_sem,
):
    moves = [
        (win_hbm, win_ref), (wout_hbm, wout_ref), (bias_hbm, bias_ref), (diff_hbm, diff_ref), (table_hbm, table_ref),
        (bg_hbm, bg_ref), (pert_hbm, pert_ref), (index_hbm, index_ref), (cutoff_hbm, cutoff_ref), (zonal_hbm, zonal_ref),
        (base_hbm, base_ref), (turn_hbm.at[lax.axis_index("lon")], turn_ref),
    ]
    moves = [pltpu.make_async_copy(src, dst, sems.at[i]) for i, (src, dst) in enumerate(moves)]
    for move in moves:
        move.start()
    lat, lon = lax.axis_index("lat"), lax.axis_index("lon")
    polar = is_polar()
    here = lax.rem(lon, PLANE)
    first = lon - here
    owner = here < OWNERS
    partner = lax.rem(lon + PLANE, N_LON)
    barrier = pltpu.get_barrier_semaphore()
    left, right = lax.rem(lon + N_LON - 1, N_LON), lax.rem(lon + 1, N_LON)
    around = (left, lon, right)

    def greet(lat_to, lon_to):
        pl.semaphore_signal(barrier, inc=1, device_id=(lat_to, lon_to), device_id_type=MESH)

    @pl.when(polar & owner)
    def _():
        def tell(d, carry):
            greet(lat, first + lax.rem(here + d, PLANE))
            return carry

        lax.fori_loop(1, PLANE, tell, 0)
        greet(lat, partner)

    greet(lat, left)
    greet(lat, right)

    @pl.when(lat > 0)
    def _():
        for to in around:
            greet(lat - 1, to)

    @pl.when(lat < N_LAT - 1)
    def _():
        for to in around:
            greet(lat + 1, to)

    for move in moves[:5]:
        move.wait()
    col = iota((C, 160), 1)
    cols_in = one_hot(jnp.where(col < 144, col >> 3, 0) == iota((C, 160), 0))
    a_in[...] = diag8(dot(dot_nt(spread_rows(HID), win_ref[...]).astype(BF16), cols_in))
    for i, part in enumerate(split(0.5 * wout_ref[...])):
        a_out[i] = diag8(dot(dot(spread_rows(C), part).astype(BF16), spread_cols(HID)))
    for h in range(HID):
        bias_tile[8 * h : 8 * h + 8, :] = jnp.full((8, R), bias_ref[h], F32)
    for c in range(C):
        d_ref[c] = jnp.full((8, R), diff_ref[c], F32)

    for move in moves[5:]:
        move.wait()
    surf = jnp.zeros((L, R), F32)
    index = index_ref[...]
    for s in range(16):
        surf = jnp.where(index == s, table_ref[s], surf)
    pf[:, 0:L, :] = pert_ref[...].astype(F32)
    pf[0, 0:L, :] = pert_ref[0].astype(F32) + surf
    pf[:, L:LP, :] = jnp.zeros((C, LP - L, R), F32)
    bf[:, 0:L, :] = bg_ref[...].astype(F32)
    bf[:, L:LP, :] = jnp.zeros((C, LP - L, R), F32)
    row_ref[0] = jnp.broadcast_to(zonal_ref[...], (8, R))
    row_ref[1] = jnp.broadcast_to(cutoff_ref[...].astype(F32), (8, R))
    basis_ref[...] = base_ref[0] * turn_ref[0:1, :] + base_ref[1] * turn_ref[1:2, :]

    lane = iota((LP, R), 1)

    def columns(p, carry):
        start = pl.multiple_of(p * 16, 16)
        xb = pack16(bf[:, pl.ds(start, 16), :]).astype(BF16)
        xb = jnp.concatenate([xb, jnp.zeros((16, 2 * R), BF16)], axis=0)
        pre = dot(a_in[...], xb)
        b = bias_tile[...]
        active = jnp.tanh(pre + jnp.concatenate([b, b], axis=1))
        slope = 1.0 - active * active
        slope_ref[:, pl.ds(start, 8), :] = slope[:, :R].reshape(HID, 8, R)
        slope_ref[:, pl.ds(start + 8, 8), :] = slope[:, R:].reshape(HID, 8, R)
        xp = pack16(pf[:, pl.ds(start, 16), :])
        top = xp[0:8]
        rest = top - top.astype(BF16).astype(F32)
        last = rest - rest.astype(BF16).astype(F32)
        xp = jnp.concatenate([xp, rest, last], axis=0).astype(BF16)
        high, low = split(slope * dot(a_in[...], xp))
        part = dot(a_out[0], high) + dot(a_out[0], low) + dot(a_out[1], high)
        mixed[:, pl.ds(start, 8), :] = part[:, :R].reshape(C, 8, R)
        mixed[:, pl.ds(start + 8, 8), :] = part[:, R:].reshape(C, 8, R)
        for i in range(3):
            c = 3 * p + i
            x = pf[c]
            image_ref[c] = x + diffusion(x, row_ref, d_ref[c], lane)
        return carry

    lax.fori_loop(0, LP // 16, columns, 0, unroll=U_FWD)

    @pl.when(jnp.logical_not(is_polar()))
    def _():
        image_ref[...] += mixed[...]

    @pl.when(is_polar())
    def _():
        bt = jnp.concatenate([basis_ref[...], jnp.zeros((R - LP, R), F32)], axis=0).T
        bt_high, bt_low = split(bt[:, :LP])
        select = pair_select()
        lane64 = iota((8, R), 1) & 63

        def spectra(q, carry):
            x = []
            for h in range(2):
                x.append(image_ref[2 * q + h] + mixed[2 * q + h])
                image_ref[2 * q + h] = x[h]
            high, low = split(jnp.concatenate(x, axis=1))
            high = dot(high, select).astype(BF16)
            low = dot(low, select).astype(BF16)
            s = dot(bt_high, high) + dot(bt_high, low) + dot(bt_low, high)
            for i, (big, small) in enumerate(FOLD):
                at = 64 * big[0] + 8 * big[1]
                tile = s[at : at + 8, :]
                if small is not None:
                    at = 64 * small[0] + 8 * small[1]
                    moved = pltpu.roll(s[at : at + 8, :], 64 - WIDTH[small[1]], 1)
                    tile = jnp.where(lane64 < WIDTH[big[1]], tile, moved)
                n = q * len(FOLD) + i
                spec_ref[n // PER_OWNER, n % PER_OWNER] = tile
            return carry

        lax.fori_loop(0, PAIRS, spectra, 0, unroll=U_SPEC)
        for i in range(TILES, SLOTS):
            spec_ref[i // PER_OWNER, i % PER_OWNER] = jnp.zeros((8, R), F32)

    sides = (lat > 0).astype(jnp.int32) + (lat < N_LAT - 1).astype(jnp.int32)
    owners = polar.astype(jnp.int32) * OWNERS
    pl.semaphore_wait(barrier, 2 + 3 * sides + owners)

    def remote(src, dst, send, recv, lat_to, lon_to):
        return pltpu.make_async_remote_copy(
            src_ref=src, dst_ref=dst, send_sem=send, recv_sem=recv, device_id=(lat_to, lon_to), device_id_type=MESH
        )

    def wait(ref, sem):
        pltpu.make_async_copy(ref, ref, sem).wait()

    @pl.when(polar)
    def _():
        def scatter(o, carry):
            @pl.when(o != here)
            def _():
                remote(spec_ref.at[o], parts.at[here], send_sem.at[0], rs_sem, lat, first + o).start()

            return carry

        lax.fori_loop(0, OWNERS, scatter, 0)

        @pl.when(owner)
        def _():
            pltpu.make_async_copy(spec_ref.at[here], parts.at[here], own_sem.at[0]).start()

    row8, lane8 = iota((8, R), 0), iota((8, R), 1)
    edge = ((lane8 == 0) & (row8 < 2)) | ((lane8 == R - 1) & (row8 >= 2) & (row8 < 4))
    pick_image = jnp.where(edge & ((row8 & 1) == 0), 1.0, 0.0)
    pick_pert = jnp.where(edge & ((row8 & 1) == 1), 1.0, 0.0)
    top = lax.Precision.HIGHEST
    for c in range(C):
        x = image_ref[c]
        lonmsg_ref[0, 0, c : c + 1, :] = x[0:1, :]
        lonmsg_ref[0, 1, c : c + 1, :] = x[LP - 1 : LP, :]
        lonmsg_ref[1, 0, c : c + 1, :] = x[L - 1 : L, :]
        lonmsg_ref[1, 1, c : c + 1, :] = x[L : L + 1, :]
        cut = dot_nt(pick_image, x, top) + dot_nt(pick_pert, (d_ref[c][None] * rows(pf[c])).reshape(LP, R), top)
        for e in range(4):
            latmsg_ref[e // 2, e % 2, c : c + 1, 0:LP] = cut[e : e + 1, :]

    remote(lonmsg_ref.at[1], lonrecv_ref.at[0], send_sem.at[1], lon_sem, lat, right).start()
    remote(lonmsg_ref.at[0], lonrecv_ref.at[1], send_sem.at[1], lon_sem, lat, left).start()

    @pl.when(lat > 0)
    def _():
        for i, to in enumerate(around):
            remote(latmsg_ref.at[0], latrecv_ref.at[1, 2 - i], send_sem.at[2], lat_sem.at[1], lat - 1, to).start()

    @pl.when(lat < N_LAT - 1)
    def _():
        for i, to in enumerate(around):
            remote(latmsg_ref.at[1], latrecv_ref.at[0, 2 - i], send_sem.at[3], lat_sem.at[0], lat + 1, to).start()

    part = split(0.5 * wout_ref[...])
    col_c = spread_cols(C)
    for i in range(2):
        a_back[i] = diag8(dot(dot_nt(spread_rows(HID), part[i]).astype(BF16), col_c))
    a_last[...] = diag8(dot(dot(spread_rows(C), win_ref[...]).astype(BF16), spread_cols(HID)))

    @pl.when(polar)
    def _():
        row, col = iota((R, R), 0), iota((R, R), 1)
        pick = one_hot(row == polar_row(col & 63))
        cut = dot(row_ref[1].astype(BF16), pick)[0:1, :]
        wave = ((row & 63) + 1).astype(F32)
        ratio = cut / wave
        g = jnp.where(wave > cut, 1.0 - ratio * ratio, 0.0)
        g_ref[0] = g * (2.0 / LONGITUDE_COUNT)
        g_ref[1] = g * (2.0 - g) * (2.0 / LONGITUDE_COUNT)
        b_ref[0], b_ref[1] = split(basis_ref[...])
        back_ref[...] = pair_select_back()

    @pl.when(polar & owner)
    def _():
        wait(parts.at[pl.ds(0, PLANE - 1)], rs_sem)
        wait(parts.at[0], own_sem.at[0])

        def add(i, acc):
            return acc + parts[i]

        total[0] = lax.fori_loop(1, PLANE, add, parts[0], unroll=True)
        remote(total.at[0], total.at[1], send_sem.at[5], pair_sem, lat, partner).start()
        wait(total.at[1], pair_sem)
        total[2] = total[0] + total[1]

        def gather(d, carry):
            to = first + lax.rem(here + d, PLANE)
            remote(total.at[2], full_ref.at[here], send_sem.at[4], ag_sem, lat, to).start()
            return carry

        lax.fori_loop(1, PLANE, gather, 0)
        pltpu.make_async_copy(total.at[2], full_ref.at[here], own_sem.at[1]).start()

    wait(lonrecv_ref, lon_sem)
    wait(lonrecv_ref, send_sem.at[1])

    @pl.when(lat > 0)
    def _():
        wait(latrecv_ref.at[0], lat_sem.at[0])
        wait(latrecv_ref.at[0], send_sem.at[2])

    @pl.when(lat < N_LAT - 1)
    def _():
        wait(latrecv_ref.at[1], lat_sem.at[1])
        wait(latrecv_ref.at[1], send_sem.at[3])

    lane24 = iota((24, R), 1)
    live = iota((24, R), 0) < C

    def neighbours(side, own):
        image, pert = [[latrecv_ref[side, i, kind] for i in range(3)] for kind in range(2)]
        fix = jnp.where(lane24 < L, pert[1], 0.0)
        fix = jnp.where(lane24 == L, pltpu.roll(pert[2], L, 1), fix)
        fix = jnp.where(lane24 == LP - 1, pltpu.roll(pert[0], LP - L, 1), fix)
        halo = image[1] + own
        halo = halo + jnp.where(lane24 == 0, pltpu.roll(image[0], R - L, 1), 0.0)
        halo = halo + jnp.where(lane24 == L - 1, pltpu.roll(image[2], R - (LP - L), 1), 0.0)
        halo = jnp.where(lane24 < L, halo, 0.0)
        there = (lat > 0) if side == 0 else (lat < N_LAT - 1)
        return jnp.where(live & there, fix, 0.0), jnp.where(live & there, halo, 0.0)

    down_fix, down_halo = neighbours(0, latmsg_ref[0, 1])
    up_fix, up_halo = neighbours(1, latmsg_ref[1, 1])
    corr[...] = jnp.concatenate([down_fix, up_fix, down_halo, up_halo, jnp.zeros((32, R), F32)], axis=0).T

    lane = iota((LP, R), 1)
    row8 = iota((8, R), 0)

    def at_edges(c, first):
        low = corr[0:LP, first + c : first + c + 1]
        high = corr[0:LP, first + 24 + c : first + 25 + c]
        return jnp.where(lane == 0, low, jnp.where(lane == R - 1, high, 0.0))

    for c in range(C):
        adj[c] = image_ref[c] + at_edges(c, 0)
        adj[c, 0:8, :] += jnp.where(row8 == 0, lonrecv_ref[0, 1, c : c + 1, :], 0.0)
        end = jnp.where(row8 == 1, lonrecv_ref[1, 1, c : c + 1, :], 0.0)
        end = jnp.where(row8 == 2, lonrecv_ref[1, 0, c : c + 1, :], end)
        end = jnp.where(row8 == 7, lonrecv_ref[0, 0, c : c + 1, :], end)
        adj[c, LP - 8 : LP, :] += end

    polar_half = (lat == N_LAT - 1).astype(jnp.int32)

    def half_columns(half, first):
        at_low, at_high = half * 64, (1 - half) * 64

        def two(x, y):
            mask = lax.broadcasted_iota(jnp.int32, x.shape, x.ndim - 1) < 64
            return jnp.where(mask, pltpu.roll(x, at_low, x.ndim - 1), pltpu.roll(y, at_high, y.ndim - 1))

        def packed(ref, n, start):
            t = [ref[:, pl.ds(start + 8 * j, 8), :].reshape(8 * n, R) for j in range(4)]
            return jnp.concatenate([two(t[0], t[1]), two(t[2], t[3])], axis=1)

        def body(p, carry):
            start = pl.multiple_of(p * 32, 32)
            high, low = split(packed(adj, C, start))
            hidden = dot(a_back[0], high) + dot(a_back[0], low) + dot(a_back[1], high)
            high, low = split(hidden * packed(slope_ref, HID, start))
            out = dot(a_last[...], high) + dot(a_last[...], low)
            for j in range(4):
                tile = pltpu.roll(out[:, (j // 2) * R : (j // 2 + 1) * R], at_high if j % 2 else at_low, 1).reshape(C, 8, R)
                rows8 = pl.ds(start + 8 * j, 8)
                if not first:
                    mask = (lax.broadcasted_iota(jnp.int32, (C, 8, R), 2) >> 6) == half
                    tile = jnp.where(mask, tile, part_ref[:, rows8, :])
                part_ref[:, rows8, :] = tile
            return carry

        lax.fori_loop(0, LP // 32, body, 0, unroll=U_ADJ)

    half_columns(1 - polar_half, True)

    @pl.when(polar & owner)
    def _():
        wait(full_ref.at[pl.ds(0, OWNERS - 1)], ag_sem)
        wait(total.at[2], own_sem.at[1])
        wait(total.at[0], send_sem.at[5])
        wait(parts.at[pl.ds(0, PLANE - 1)], send_sem.at[4])
        wait(full_ref.at[pl.ds(0, OWNERS - 1)], send_sem.at[0])

    @pl.when(polar & jnp.logical_not(owner))
    def _():
        wait(full_ref, ag_sem)
        wait(full_ref, send_sem.at[0])

    @pl.when(jnp.logical_not(is_polar()))
    def _():
        tangent_ref[...] = adj[:, 0:L, :].astype(BF16)

    @pl.when(is_polar())
    def _():
        g_tangent, g_adjoint = g_ref[0], g_ref[1]
        b_high, b_low = b_ref[0], b_ref[1]
        back = back_ref[...]

        def rebuild(q, carry):
            tiles = {}
            for i, (big, small) in enumerate(FOLD):
                tile = tile_of(full_ref, q * len(FOLD) + i)
                tiles[big] = tile
                if small is not None:
                    tiles[small] = pltpu.roll(tile, R - 64 + WIDTH[small[1]], 1)
            s = jnp.concatenate([tiles[kind, a] for kind in (0, 1) for a in range(8)], axis=0)
            high, low = split(jnp.concatenate([g_tangent * s, g_adjoint * s], axis=1))
            removed = dot(b_high, high) + dot(b_high, low) + dot(b_low, high)
            removed = jnp.concatenate([removed[:, :R], removed[:, R:]], axis=0)
            high, low = split(removed)
            removed = dot(high, back) + dot(low, back)
            for h in range(2):
                c = 2 * q + h
                x = adj[c]
                lanes = slice(h * R, (h + 1) * R)
                tangent_ref[c] = (x - removed[:LP, lanes])[0:L].astype(BF16)
                adj[c] = x - removed[LP:, lanes]
            return carry

        lax.fori_loop(0, PAIRS, rebuild, 0, unroll=U_REB)

    tangent_out = pltpu.make_async_copy(tangent_ref, tangent_hbm, out_sems.at[0])
    tangent_out.start()

    half_columns(polar_half, False)
    outs = [tangent_out]

    for c in range(C):
        x = adj[c]
        out = x + diffusion(x, row_ref, d_ref[c], lane, at_edges(c, 48)) + part_ref[c]
        gradient_ref[c] = out[0:L].astype(BF16)
        if c % 6 == 5:
            part = pl.ds(c - 5, 6)
            outs.append(pltpu.make_async_copy(gradient_ref.at[part], gradient_hbm.at[part], out_sems.at[1 + c // 6]))
            outs[-1].start()
    for move in outs:
        move.wait()


def settle_kernel(tangent_ref, gradient_ref, tangent_out, gradient_out, held, sems):
    ends = ((tangent_ref, tangent_out), (gradient_ref, gradient_out))
    half = C // 2
    parts = [(i, pl.ds(h * half, half)) for i in range(2) for h in range(2)]
    loads = [pltpu.make_async_copy(ends[i][0].at[p], held.at[i, p], sems.at[0, n]) for n, (i, p) in enumerate(parts)]
    stores = [pltpu.make_async_copy(held.at[i, p], ends[i][1].at[p], sems.at[1, n]) for n, (i, p) in enumerate(parts)]
    for load in loads:
        load.start()
    for load, store in zip(loads, stores):
        load.wait()
        store.start()
    for store in stores:
        store.wait()


def hbm():
    return pl.BlockSpec(memory_space=pltpu.HBM)


def anywhere():
    return pl.BlockSpec(memory_space=pl.ANY)


LIMIT = 58 * 2**20


def per_device(
    background_state,
    perturbation,
    surface_pattern_index,
    surface_amplitude_table,
    cutoff,
    zonal_row_weight,
    diffusivity,
    input_weight,
    bias,
    output_weight,
):
    base, turn = (jnp.asarray(t) for t in base_tables())
    shape = jax.ShapeDtypeStruct
    scratch = pltpu.VMEM
    field = scratch((C, LP, R), F32)
    message = scratch((2, 2, 24, R), F32)
    dma = pltpu.SemaphoreType.DMA
    tangent, gradient = pl.pallas_call(
        step_kernel,
        out_shape=(shape((C, L, R), BF16), shape((C, L, R), BF16)),
        in_specs=[hbm()] * 12,
        out_specs=(hbm(), hbm()),
        scratch_shapes=[
            scratch((C, L, R), BF16),
            scratch((C, L, R), BF16),
            dma((4,)),
            field,
            scratch((HID, LP, R), F32),
            scratch((OWNERS, PER_OWNER, 8, R), F32),
            field,
            scratch((C, 8, R), F32),
            scratch((2, 8, R), F32),
            scratch((C, HID), BF16),
            scratch((C, HID), F32),
            scratch((LP, R), F32),
            scratch((C, L, R), BF16),
            scratch((C, L, R), BF16),
            scratch((L, R), jnp.int32),
            pltpu.SMEM((16,), F32),
            scratch((1, R), jnp.int32),
            scratch((1, R), F32),
            pltpu.SMEM((C,), F32),
            pltpu.SMEM((HID,), F32),
            scratch((2, LP, R), F32),
            scratch((2, R), F32),
            field,
            scratch((8 * HID, R), F32),
            scratch((8 * HID, 160), BF16),
            scratch((2, 8 * C, 8 * HID), BF16),
            field,
            dma((12,)),
            scratch((OWNERS, PER_OWNER, 8, R), F32),
            message,
            scratch((2, 3, 2, 24, R), F32),
            message,
            scratch((2, 8 * HID, 8 * C), BF16),
            scratch((8 * C, 8 * HID), BF16),
            scratch((2, LP, R), BF16),
            scratch((R, 2 * R), BF16),
            scratch((2, R, R), F32),
            scratch((PLANE, PER_OWNER, 8, R), F32),
            scratch((3, PER_OWNER, 8, R), F32),
            message,
            field,
            field,
            scratch((R, R), F32),
            dma((6,)),
            dma,
            dma((2,)),
            dma,
            dma,
            dma((2,)),
            dma,
        ],
        compiler_params=pltpu.CompilerParams(collective_id=0, has_side_effects=True, vmem_limit_bytes=LIMIT),
        name="step",
    )(
        background_state, perturbation, surface_pattern_index, surface_amplitude_table, cutoff.reshape(1, R),
        zonal_row_weight.reshape(1, R), diffusivity, input_weight.T, bias, output_weight, base, turn,
    )
    return pl.pallas_call(
        settle_kernel,
        out_shape=(shape((C, L, R), BF16), shape((C, L, R), BF16)),
        in_specs=[hbm()] * 2,
        out_specs=(hbm(), hbm()),
        scratch_shapes=[scratch((2, C, L, R), BF16), dma((2, 4))],
        compiler_params=pltpu.CompilerParams(vmem_limit_bytes=LIMIT),
        name="settle",
    )(tangent, gradient)


def solution(mesh):
    placed = (
        P(None, "lon", "lat"),
        P(None, "lon", "lat"),
        P("lon", "lat"),
        P(),
        P("lat"),
        P("lat"),
        P(),
        P(),
        P(),
        P(),
    )
    return jax.shard_map(
        per_device,
        mesh=mesh,
        in_specs=placed,
        out_specs=(P(None, "lon", "lat"), P(None, "lon", "lat")),
        check_vma=False,
    )
```
